512 devices in a mesh: rows: 32 (over y, x, core), sub: 16 (over z).
Axes of the slice: x: 4, y: 4, z: 16, core: 2. Of those that a mesh axis runs over, the one named last changes fastest.
Arguments:
- knobs: float32 [48, 1048576], P(None, ('rows', 'sub')), may hold values from -6 to 6
- lengthscale: float32 [48], replicated, may hold values from 4 to 16
- earlier: float32 [256, 1048576], P(None, ('rows', 'sub')), may hold values from -0.06 to 0.06
- diagonal: float32 [1048576], P(('rows', 'sub')), may hold values from 1 to 2
- pivots: int32 [2, 128], replicated, may hold values from 0 to 1048575, as said below
Outputs:
- new_factor: float32 [256, 1048576], P(None, ('rows', 'sub'))
- residual_diag: float32 [1048576], P(('rows', 'sub'))
The draws below stay inside these ranges and needn't reach their ends.
Inputs may be any that keep to these rules, and one draw needn't show every extreme that they name: All 256 ids are distinct row ids; the owners of the rows are chosen unevenly, some devices holding many pivots and most none.
All inputs are finite; a program needn't handle non-finite values.
Results may differ from the reference program's by a relative error of at most 0.0003.
Values sent between devices are 32-bit elements; how exact they have to be, the bound alone decides.
A program may use at most 64 MiB of HBM per device.

```python
import math
import jax
import jax.numpy as jnp
from jax import lax

KNOBS = 48
BLOCK = 128
PREV = 256
CANDIDATE_LINES = 2048
TOTAL = 1048576
N_ROWS = 32
N_SUB = 16


def draw_pivots(key, part):
    key = jax.random.fold_in(key, 11)
    overall_number = CANDIDATE_LINES * N_ROWS * N_SUB
    holder_units = overall_number // CANDIDATE_LINES
    initial_seed_handle, key_b = jax.random.split(key)
    extra_weight = jax.random.randint(initial_seed_handle, (holder_units,), 0, 512)
    nugget_spread = jax.random.randint(key_b, (overall_number,), 0, 512)
    chosen_position = jnp.arange(overall_number, dtype=jnp.int32)
    selection_merit = (nugget_spread + jnp.repeat(extra_weight, CANDIDATE_LINES)) * overall_number + chosen_position
    selection_merit = selection_merit.at[0].set(1024 * overall_number)
    selection_merit = selection_merit.at[overall_number - 1].set(1024 * overall_number + overall_number - 1)
    values, chosen = lax.top_k(selection_merit, 2 * BLOCK)
    return (values % overall_number).astype(jnp.int32).reshape(2, BLOCK)


def draw_earlier(key, part):
    key = jax.random.fold_in(key, 23)
    overall_number = CANDIDATE_LINES * N_ROWS * N_SUB
    values = jnp.clip(0.02 * jax.random.normal(key, (PREV, overall_number), jnp.float32), -0.06, 0.06)
    return values.astype(jnp.float32)


def levels(own_key, shape, shards, low, high):
    gain = 1.0
    for position, shards_of in shards:
        heights = jax.random.uniform(jax.random.fold_in(jax.random.fold_in(own_key, 6), position), (shards_of,), jnp.float32, low / len(shards), high / len(shards))
        gain = gain * jnp.repeat(jnp.exp(heights), shape[position] // shards_of).reshape((-1,) + (1,) * (len(shape) - 1 - position))
    return gain


def scatter_about(key, extent, spread, reach, cuts=(), kind=jnp.bfloat16):
    array = jax.random.normal(key, extent, jnp.float32) * spread
    if len(cuts) > 0:
        array = levels(key, extent, cuts, -0.22, 0.18) * array
    return jnp.clip(array, min=-reach, max=reach).astype(kind)


def setup_inputs(seed: int = 0) -> dict:
    splits = jax.random.split(jax.random.key(seed), 6)
    return {
        "knobs": scatter_about(splits[0], (KNOBS, TOTAL), 1.0, 6.0, ((1, 512),), jnp.float32),
        "lengthscale": jnp.clip(jnp.exp(jax.random.uniform(splits[1], (KNOBS,), jnp.float32, math.log(4.0), math.log(16.0))), 4.0, 16.0),
        "earlier": draw_earlier(jax.random.fold_in(splits[5], 71), 0),
        "diagonal": jnp.clip(1.0 + 1.0 * jax.random.uniform(splits[3], (TOTAL,), jnp.float32) ** levels(splits[3], (TOTAL,), ((0, 512),), -0.2, 0.2), 1.0, 2.0),
        "pivots": draw_pivots(jax.random.fold_in(splits[5], 71), 0),
    }


def kern(left, right_block):
    cross_product = jnp.dot(left.T.astype(jnp.float32), right_block.astype(jnp.float32), precision=lax.Precision.HIGHEST, preferred_element_type=jnp.float32)
    lengthscale_square = jnp.sum(left * left, axis=0)
    right_square_norm = jnp.sum(right_block * right_block, axis=0)
    return jnp.exp(-0.5 * (lengthscale_square[:, None] + right_square_norm[None, :] - 2.0 * cross_product))

def product(left, right_block):
    return jnp.dot(left.T.astype(jnp.float32), right_block.astype(jnp.float32), precision=lax.Precision.HIGHEST, preferred_element_type=jnp.float32)

def factor_block(scaled, pivot_ids, pairs):
    piv = scaled[:, pivot_ids]
    tile = kern(piv, scaled)
    square = kern(piv, piv)
    for columns in pairs:
        at_piv = columns[:, pivot_ids]
        tile = tile - product(at_piv, columns)
        square = square - product(at_piv, at_piv)
    square = square + 0.5 * jnp.eye(square.shape[0], dtype=jnp.float32)
    lower = jnp.linalg.cholesky(square)
    return lax.linalg.triangular_solve(lower, tile, left_side=True, lower=True)

def reference(knobs, lengthscale, earlier, diagonal, pivots):
    scaled = knobs / lengthscale[:, None]
    first = factor_block(scaled, pivots[0], [earlier])
    second = factor_block(scaled, pivots[1], [earlier, first])
    residual_diag = diagonal - jnp.sum(first * first, axis=0) - jnp.sum(second * second, axis=0)
    return (jnp.concatenate([first, second], axis=0), residual_diag)
```

```python
import jax
import jax.numpy as jnp
from jax import lax
from jax.experimental import pallas as pl
from jax.experimental.pallas import tpu as pltpu
from jax.sharding import PartitionSpec as P

MESH = pl.DeviceIdType.MESH
KNOBS, PREV, PIVOTS, LANES = 48, 256, 256, 128
TABLE = KNOBS + PREV
PIECES = 32
PIECE_ROWS = TABLE * (PIVOTS // LANES) // PIECES
CHUNK = 512
PANEL = 8
OUTER = 64
F32, BF16 = jnp.float32, jnp.bfloat16


def split_two(x):
    high = x.astype(BF16)
    return high, (x - high.astype(F32)).astype(BF16)


def split_three(x):
    high = x.astype(BF16)
    rest = x - high.astype(F32)
    mid = rest.astype(BF16)
    return high, mid, (rest - mid.astype(F32)).astype(BF16)


def dot(left, right, dims=((1,), (0,))):
    return lax.dot_general(left, right, (dims, ((), ())), preferred_element_type=F32)


def column_of(row):
    count = row.shape[1]
    square = jnp.broadcast_to(row, (count, count))
    same = lax.broadcasted_iota(jnp.int32, (count, count), 0) == lax.broadcasted_iota(
        jnp.int32, (count, count), 1
    )
    return jnp.sum(jnp.where(same, square, 0.0), axis=1, keepdims=True)


def select_kernel(ids_ref, ls_ref, knobs_ref, earlier_ref, out_ref, acc_ref):
    step = pl.program_id(0)
    width = knobs_ref.shape[1]
    count = width * pl.num_programs(0)
    device = lax.axis_index("rows") * lax.axis_size("sub") + lax.axis_index("sub")
    ids = jnp.concatenate([ids_ref[0:1, :], ids_ref[1:2, :]], axis=1) - (device * count + step * width)
    hot = jnp.where(lax.broadcasted_iota(jnp.int32, (width, PIVOTS), 0) == ids, 1.0, 0.0).astype(BF16)
    scaled = knobs_ref[...] / column_of(ls_ref[...])
    table = jnp.concatenate([scaled, earlier_ref[...]], axis=0)
    high, mid, low = split_three(table)
    found = dot(high, hot) + dot(mid, hot) + dot(low, hot)

    @pl.when(step == 0)
    def _():
        acc_ref[...] = found

    @pl.when(step > 0)
    def _():
        acc_ref[...] += found

    @pl.when(step == pl.num_programs(0) - 1)
    def _():
        for piece in range(PIECES):
            row, half = (piece // 2) * PIECE_ROWS, (piece % 2) * LANES
            out_ref[piece] = acc_ref[row : row + PIECE_ROWS, half : half + LANES]


def gather_kernel(part_ref, whole_ref, rows_in, near_in, far_in, near_out, far_out,
                  send_a, recv_a, send_b, recv_b, send_c, recv_c, send_d, recv_d):
    rows, sub = lax.axis_size("rows"), lax.axis_size("sub")
    row, z = lax.axis_index("rows"), lax.axis_index("sub")
    group = 4
    low, high = lax.rem(z, group), lax.div(z, group)

    def row_partner(k):
        return (lax.rem(row + k, rows), z)

    def near_partner(k):
        return (row, high * group + lax.rem(low + k, group))

    def far_partner(k):
        return (row, lax.rem(z + k * group, sub))

    barrier = pltpu.get_barrier_semaphore()

    def greet(k, _):
        pl.semaphore_signal(barrier, inc=1, device_id=row_partner(k), device_id_type=MESH)
        return _

    lax.fori_loop(1, rows, greet, 0)
    for k in range(1, group):
        pl.semaphore_signal(barrier, inc=1, device_id=near_partner(k), device_id_type=MESH)
        pl.semaphore_signal(barrier, inc=1, device_id=far_partner(k), device_id_type=MESH)
    pl.semaphore_wait(barrier, rows - 1 + 2 * (group - 1))

    def scatter(k):
        partner = row_partner(k)
        return pltpu.make_async_remote_copy(
            src_ref=part_ref.at[partner[0]], dst_ref=rows_in.at[k], send_sem=send_a.at[k],
            recv_sem=recv_a.at[k], device_id=partner, device_id_type=MESH)

    lax.fori_loop(1, rows, lambda k, c: (scatter(k).start(), c)[1], 0)
    lax.fori_loop(1, rows, lambda k, c: (scatter(k).wait_recv(), c)[1], 0)
    total = part_ref[row]
    for k in range(1, PIECES):
        total = total + rows_in[k]
    near_out[...] = total

    def near(k):
        return pltpu.make_async_remote_copy(
            src_ref=near_out, dst_ref=near_in.at[k], send_sem=send_b.at[k],
            recv_sem=recv_b.at[k], device_id=near_partner(k), device_id_type=MESH)

    for k in range(1, group):
        near(k).start()
    for k in range(1, group):
        near(k).wait_recv()
    total = near_out[...] + near_in[1] + near_in[2] + near_in[3]
    far_out[...] = total

    def far(k):
        return pltpu.make_async_remote_copy(
            src_ref=far_out, dst_ref=far_in.at[k], send_sem=send_c.at[k],
            recv_sem=recv_c.at[k], device_id=far_partner(k), device_id_type=MESH)

    for k in range(1, group):
        far(k).start()
    for k in range(1, group):
        far(k).wait_recv()
    whole_ref[row] = far_out[...] + far_in[1] + far_in[2] + far_in[3]

    def spread(k):
        return pltpu.make_async_remote_copy(
            src_ref=whole_ref.at[row], dst_ref=whole_ref.at[row], send_sem=send_d.at[k],
            recv_sem=recv_d.at[k], device_id=row_partner(k), device_id_type=MESH)

    def arrival(k):
        source = lax.rem(row + rows - k, rows)
        return pltpu.make_async_remote_copy(
            src_ref=whole_ref.at[source], dst_ref=whole_ref.at[source], send_sem=send_d.at[k],
            recv_sem=recv_d.at[k], device_id=row_partner(k), device_id_type=MESH)

    lax.fori_loop(1, rows, lambda k, c: (spread(k).start(), c)[1], 0)
    lax.fori_loop(1, rows, lambda k, c: (scatter(k).wait_send(), c)[1], 0)
    for k in range(1, group):
        near(k).wait_send()
        far(k).wait_send()
    lax.fori_loop(1, rows, lambda k, c: (arrival(k).wait_recv(), c)[1], 0)
    lax.fori_loop(1, rows, lambda k, c: (spread(k).wait_send(), c)[1], 0)


def extended(scaled, axis):
    square = -0.5 * jnp.sum(scaled * scaled, axis=axis, keepdims=True)
    pieces = [p.astype(F32) for p in split_three(square)]
    shape = tuple(16 if d == axis else s for d, s in enumerate(scaled.shape))
    place = lax.broadcasted_iota(jnp.int32, shape, axis)

    def rows(values):
        out = jnp.zeros(shape, F32)
        for i, value in enumerate(values):
            out = jnp.where(place == i, value, out)
        return out.astype(BF16)

    high, low = split_two(scaled)
    return high, low, rows, pieces


def left_form(scaled):
    high, low, rows, pieces = extended(scaled, 1)
    return jnp.concatenate([high, high, low, low, rows(pieces + [1.0, 1.0, 1.0])], axis=1)


def right_form(scaled):
    high, low, rows, pieces = extended(scaled, 0)
    return jnp.concatenate([high, low, high, low, rows([1.0, 1.0, 1.0] + pieces)], axis=0)


def tile_of(kern_left, prev_left, scaled, earlier):
    tile = jnp.exp(dot(kern_left[...], right_form(scaled)))
    high, low = split_two(earlier)
    prev_high = prev_left[0]
    return tile - (dot(prev_high, high) + (dot(prev_high, low) + dot(prev_left[1], high)))


def stacked(x, order):
    parts = split_three(x)
    return jnp.concatenate([parts[i] for i in order], axis=0)


LEFT_ORDER, RIGHT_ORDER = (0, 0, 1, 1, 0, 2), (0, 1, 0, 1, 2, 0)


def factor(aug):
    size = PIVOTS
    sub = lax.broadcasted_iota(jnp.int32, (PANEL, 1), 0)
    for start in range(0, size, OUTER):
        stop = start + OUTER
        for r in range(start, stop, PANEL):
            panel = aug[r : r + PANEL, :]
            for j in range(PANEL):
                pivot = panel[j : j + 1, r + j : r + j + 1]
                scale = lax.rsqrt(pivot)
                line = panel[j : j + 1, :] * scale
                below = jnp.where(sub > j, panel[:, r + j : r + j + 1] * scale, 0.0)
                panel = jnp.where(sub == j, line, panel - below * line)
            aug[r : r + PANEL, :] = panel
            if r + PANEL < stop:
                left = stacked(panel[:, : size], LEFT_ORDER)[:, r + PANEL : stop]
                aug[r + PANEL : stop, :] -= dot(left, stacked(panel, RIGHT_ORDER), ((0,), (0,)))
        if stop < size:
            block = aug[start:stop, :]
            high, low = split_two(block)
            left = jnp.concatenate([high, high, low, low], axis=0)[:, stop:size]
            right = jnp.concatenate([high, low, high, low], axis=0)
            aug[stop:size, :] -= dot(left, right, ((0,), (0,)))


def solve_kernel(whole_ref, ls_ref, knobs_ref, earlier_ref, diag_ref, out_ref, res_ref,
                 table, aug, kern_left, prev_left, inverse):
    step = pl.program_id(0)

    @pl.when(step == 0)
    def _():
        for piece in range(PIECES):
            row, half = (piece // 2) * PIECE_ROWS, (piece % 2) * LANES
            table[row : row + PIECE_ROWS, half : half + LANES] = whole_ref[piece]
        scaled = table[:KNOBS, :]
        earlier = table[KNOBS:, :]
        kern_left[...] = left_form(scaled.T)
        prev_left[0], prev_left[1] = split_two(earlier.T)
        eye = jnp.where(
            lax.broadcasted_iota(jnp.int32, (PIVOTS, PIVOTS), 0)
            == lax.broadcasted_iota(jnp.int32, (PIVOTS, PIVOTS), 1), 1.0, 0.0)
        aug[:, :PIVOTS] = tile_of(kern_left, prev_left, scaled, earlier) + 0.5 * eye
        aug[:, PIVOTS:] = eye
        factor(aug)
        inverse[0], inverse[1] = split_two(aug[:, PIVOTS:])

    scaled = knobs_ref[...] / column_of(ls_ref[...])
    tile = tile_of(kern_left, prev_left, scaled, earlier_ref[...])
    high, low = split_two(tile)
    inv_high = inverse[0]
    new = dot(inv_high, high) + (dot(inv_high, low) + dot(inverse[1], high))
    out_ref[...] = new
    res_ref[...] = diag_ref[...] - jnp.sum(new * new, axis=0, keepdims=True)


def gather(part):
    vmem = pl.BlockSpec(memory_space=pltpu.VMEM)
    slots = lambda n: pltpu.VMEM((n, PIECE_ROWS, LANES), F32)
    dma = pltpu.SemaphoreType.DMA
    return pl.pallas_call(
        gather_kernel,
        out_shape=jax.ShapeDtypeStruct(part.shape, F32),
        in_specs=[vmem],
        out_specs=vmem,
        scratch_shapes=[
            slots(PIECES), slots(4), slots(4),
            pltpu.VMEM((PIECE_ROWS, LANES), F32), pltpu.VMEM((PIECE_ROWS, LANES), F32),
            dma((PIECES,)), dma((PIECES,)), dma((4,)), dma((4,)),
            dma((4,)), dma((4,)), dma((PIECES,)), dma((PIECES,)),
        ],
        compiler_params=pltpu.CompilerParams(
            collective_id=0, has_side_effects=True, vmem_limit_bytes=8 << 20),
        name="gather_pivots",
    )(part)


def per_device(knobs, lengthscale, earlier, diagonal, pivots):
    count = knobs.shape[1]
    steps = count // CHUNK
    scale_row = lengthscale.reshape(1, KNOBS)
    piece_shape = (PIECES, PIECE_ROWS, LANES)
    fixed = lambda *shape: pl.BlockSpec(shape, lambda i: (0,) * len(shape))
    chunk = lambda rows: pl.BlockSpec((rows, CHUNK), lambda i: (0, i))
    part = pl.pallas_call(
        select_kernel,
        out_shape=jax.ShapeDtypeStruct(piece_shape, F32),
        grid=(steps,),
        in_specs=[fixed(2, LANES), fixed(1, KNOBS), chunk(KNOBS), chunk(PREV)],
        out_specs=fixed(*piece_shape),
        scratch_shapes=[pltpu.VMEM((TABLE, PIVOTS), F32)],
        compiler_params=pltpu.CompilerParams(vmem_limit_bytes=24 << 20),
        name="select_pivots",
    )(pivots, scale_row, knobs, earlier)
    whole = gather(part)
    new_factor, residual = pl.pallas_call(
        solve_kernel,
        out_shape=(
            jax.ShapeDtypeStruct((PIVOTS, count), F32),
            jax.ShapeDtypeStruct((1, count), F32),
        ),
        grid=(steps,),
        in_specs=[fixed(*piece_shape), fixed(1, KNOBS), chunk(KNOBS), chunk(PREV), chunk(1)],
        out_specs=(chunk(PIVOTS), chunk(1)),
        scratch_shapes=[
            pltpu.VMEM((TABLE, PIVOTS), F32),
            pltpu.VMEM((PIVOTS, 2 * PIVOTS), F32),
            pltpu.VMEM((PIVOTS, 4 * KNOBS + 16), BF16),
            pltpu.VMEM((2, PIVOTS, PREV), BF16),
            pltpu.VMEM((2, PIVOTS, PIVOTS), BF16),
        ],
        compiler_params=pltpu.CompilerParams(vmem_limit_bytes=24 << 20),
        name="solve_columns",
    )(whole, scale_row, knobs, earlier, diagonal.reshape(1, count))
    return new_factor, residual.reshape(count)


def solution(mesh):
    in_specs = (P(None, ("rows", "sub")), P(), P(None, ("rows", "sub")), P(("rows", "sub")), P())
    out_specs = (P(None, ("rows", "sub")), P(("rows", "sub")))
    return jax.shard_map(
        per_device, mesh=mesh, in_specs=in_specs, out_specs=out_specs, check_vma=False
    )
```

```python
import jax
import jax.numpy as jnp
from jax import lax
from jax.experimental import pallas as pl
from jax.experimental.pallas import tpu as pltpu
from jax.sharding import PartitionSpec as P

MESH = pl.DeviceIdType.MESH
KNOBS, PREV, PIVOTS, LANES = 48, 256, 256, 128
TABLE = KNOBS + PREV
PIECES = 32
PIECE_ROWS = TABLE * (PIVOTS // LANES) // PIECES
CHUNK = 512
GROUP, BLOCK = 8, 32
F32, BF16 = jnp.float32, jnp.bfloat16


def split_two(x):
    high = x.astype(BF16)
    return high, (x - high.astype(F32)).astype(BF16)


def split_three(x):
    high = x.astype(BF16)
    rest = x - high.astype(F32)
    mid = rest.astype(BF16)
    return high, mid, (rest - mid.astype(F32)).astype(BF16)


def dot(left, right, dims=((1,), (0,))):
    return lax.dot_general(left, right, (dims, ((), ())), preferred_element_type=F32)


def column_of(row):
    count = row.shape[1]
    square = jnp.broadcast_to(row, (count, count))
    same = lax.broadcasted_iota(jnp.int32, (count, count), 0) == lax.broadcasted_iota(
        jnp.int32, (count, count), 1
    )
    return jnp.sum(jnp.where(same, square, 0.0), axis=1, keepdims=True)


def ring(step, size):
    return min(step % size, -step % size)


AROUND = sorted(
    ((y, x, c) for y in range(4) for x in range(4) for c in range(2)),
    key=lambda t: -(4 * (ring(t[0], 4) + ring(t[1], 4)) + t[2]),
)[:-1]
NEAR, FAR, OPPOSITE = (-1, 1), (-3, 3, -6, 6), 8
ALONG = NEAR + (OPPOSITE,) + FAR
PARTS = 4


def collect_kernel(ids_hbm, ls_hbm, knobs_hbm, earlier_hbm, whole_ref, ids_ref, ls_ref, knobs, earlier, part, rows_in, z_in, z_out,
                   small_sem, load_sem, send_a, recv_a, send_z, recv_z, send_d, recv_d):
    row, z = lax.axis_index("rows"), lax.axis_index("sub")
    subs = lax.axis_size("sub")
    core, x0, y0 = lax.rem(row, 2), lax.rem(lax.div(row, 2), 4), lax.div(row, 8)
    count = knobs_hbm.shape[1]
    width = count // PARTS

    def load(i):
        columns = pl.ds(i * width, width)
        return [
            pltpu.make_async_copy(hbm.at[:, columns], vmem.at[:, columns], load_sem.at[j, i])
            for j, (hbm, vmem) in enumerate(((knobs_hbm, knobs), (earlier_hbm, earlier)))
        ]

    def around(t, sign=1):
        dy, dx, dc = t
        y, x = lax.rem(y0 + (dy * sign) % 4, 4), lax.rem(x0 + (dx * sign) % 4, 4)
        return (y * 4 + x) * 2 + (core + dc - 2 * core * dc)

    def along(d):
        return lax.rem(z + d % subs, subs)

    small = [
        pltpu.make_async_copy(hbm, vmem, small_sem.at[j])
        for j, (hbm, vmem) in enumerate(((ids_hbm, ids_ref), (ls_hbm, ls_ref)))
    ]
    for copy in small:
        copy.start()
    for i in range(PARTS):
        for copy in load(i):
            copy.start()
    barrier = pltpu.get_barrier_semaphore()
    for t in AROUND:
        pl.semaphore_signal(barrier, inc=1, device_id=(around(t), z), device_id_type=MESH)
    for d in ALONG:
        pl.semaphore_signal(barrier, inc=1, device_id=(row, along(d)), device_id_type=MESH)

    for copy in small:
        copy.wait()
    device = row * subs + z
    ids = jnp.concatenate([ids_ref[0:1, :], ids_ref[1:2, :]], axis=1) - device * count
    scale = column_of(ls_ref[...])
    table = None
    for i in range(PARTS):
        for copy in load(i):
            copy.wait()
        columns = pl.ds(i * width, width)
        hot = lax.broadcasted_iota(jnp.int32, (width, PIVOTS), 0) == ids - i * width
        hot = jnp.where(hot, 1.0, 0.0).astype(BF16)
        lines = jnp.concatenate([knobs[:, columns] / scale, earlier[:, columns]], axis=0)
        high, mid, low = split_three(lines)
        found = dot(high, hot) + dot(mid, hot) + dot(low, hot)
        table = found if table is None else table + found
    for piece in range(PIECES):
        top, half = (piece // 2) * PIECE_ROWS, (piece % 2) * LANES
        part[piece] = table[top : top + PIECE_ROWS, half : half + LANES]
    pl.semaphore_wait(barrier, len(AROUND) + len(ALONG))

    def scatter(i):
        target = around(AROUND[i])
        return pltpu.make_async_remote_copy(
            src_ref=part.at[target], dst_ref=rows_in.at[i], send_sem=send_a.at[i], recv_sem=recv_a.at[i],
            device_id=(target, z), device_id_type=MESH)

    def pass_on(i, source):
        return pltpu.make_async_remote_copy(
            src_ref=z_out.at[source], dst_ref=z_in.at[i], send_sem=send_z.at[i], recv_sem=recv_z.at[i],
            device_id=(row, along(ALONG[i])), device_id_type=MESH)

    def spread(i, source):
        return pltpu.make_async_remote_copy(
            src_ref=whole_ref.at[source], dst_ref=whole_ref.at[source], send_sem=send_d.at[i],
            recv_sem=recv_d.at[i], device_id=(around(AROUND[i]), z), device_id_type=MESH)

    others = range(len(AROUND))
    first, second = range(len(NEAR) + 1), range(len(NEAR) + 1, len(ALONG))
    for i in others:
        scatter(i).start()
    total = part[row]
    for i in reversed(others):
        scatter(i).wait_recv()
        total = total + rows_in[i]
    z_out[0] = total
    for i in first:
        pass_on(i, 0).start()
    for i in range(len(NEAR)):
        pass_on(i, 0).wait_recv()
        total = total + z_in[i]
    z_out[1] = total
    for i in second:
        pass_on(i, 1).start()
    for i in others:
        scatter(i).wait_send()
    for i in second:
        pass_on(i, 1).wait_recv()
        total = total + z_in[i]
    pass_on(len(NEAR), 0).wait_recv()
    whole_ref[row] = total + z_in[len(NEAR)]
    for i in others:
        spread(i, row).start()
    for i in first:
        pass_on(i, 0).wait_send()
    for i in second:
        pass_on(i, 1).wait_send()
    for i in reversed(others):
        spread(i, around(AROUND[i], -1)).wait_recv()
    for i in others:
        spread(i, row).wait_send()


def extended(scaled, axis):
    square = -0.5 * jnp.sum(scaled * scaled, axis=axis, keepdims=True)
    pieces = [p.astype(F32) for p in split_three(square)]
    shape = tuple(16 if d == axis else s for d, s in enumerate(scaled.shape))
    place = lax.broadcasted_iota(jnp.int32, shape, axis)

    def rows(values):
        out = jnp.zeros(shape, F32)
        for i, value in enumerate(values):
            out = jnp.where(place == i, value, out)
        return out.astype(BF16)

    high, low = split_two(scaled)
    return high, low, rows, pieces


def left_form(scaled):
    high, low, rows, pieces = extended(scaled, 1)
    return jnp.concatenate([high, high, low, low, rows(pieces + [1.0, 1.0, 1.0])], axis=1)


def right_form(scaled):
    high, low, rows, pieces = extended(scaled, 0)
    return jnp.concatenate([high, low, high, low, rows([1.0, 1.0, 1.0] + pieces)], axis=0)


def tile_of(kern_left, prev_left, scaled, earlier):
    tile = jnp.exp(dot(kern_left[...], right_form(scaled)))
    high, low = split_two(earlier)
    prev_high = prev_left[0]
    return tile - (dot(prev_high, high) + (dot(prev_high, low) + dot(prev_left[1], high)))


def factor(square):
    size = PIVOTS
    sub = lax.broadcasted_iota(jnp.int32, (GROUP, LANES), 0)
    sub_wide = lax.broadcasted_iota(jnp.int32, (GROUP, size), 0)
    lane_wide = lax.broadcasted_iota(jnp.int32, (GROUP, size), 1)
    full = lambda v: jnp.broadcast_to(v, (GROUP, LANES))
    wide = lambda v: jnp.concatenate([v] * (size // LANES), axis=1)
    groups = BLOCK // GROUP
    for start in range(0, size, BLOCK):
        stop = start + BLOCK
        lines = [square[start + GROUP * q : start + GROUP * q + GROUP, :] for q in range(groups)]
        for g in range(groups):
            first = start + GROUP * g
            below = range(g + 1, groups)
            cols = [
                {q: full(lines[q][:, first + k : first + k + 1]) for q in range(g, groups)} for k in range(GROUP)
            ]
            here = (lane_wide >= first) & (lane_wide < first + GROUP)
            for q in range(groups):
                fresh = jnp.where(lane_wide - first == sub_wide, 1.0, 0.0) if q == g else 0.0
                lines[q] = jnp.where(here, fresh, lines[q])
            for j in range(GROUP):
                scale = lax.rsqrt(full(cols[j][g][j : j + 1, :]))
                factors = {q: cols[j][q] * scale for q in below}
                factors[g] = jnp.where(sub > j, cols[j][g] * scale, 0.0)
                for k in range(j + 1, GROUP):
                    entry = full(cols[k][g][j : j + 1, :]) * scale
                    for q in range(g, groups):
                        cols[k][q] = cols[k][q] - factors[q] * entry
                line = jnp.broadcast_to(lines[g][j : j + 1, :], (GROUP, size)) * wide(scale)
                lines[g] = jnp.where(sub_wide == j, line, lines[g] - wide(factors[g]) * line)
                for q in below:
                    lines[q] = lines[q] - wide(factors[q]) * line
        block = jnp.concatenate(lines, axis=0)
        square[start:stop, :] = block
        if stop < size:
            high, low = split_two(block)
            left = jnp.concatenate([high, high, low, low], axis=0)[:, stop:]
            right = jnp.concatenate([high, low, high, low], axis=0)
            change = dot(left, right, ((0,), (0,)))
            lane = lax.broadcasted_iota(jnp.int32, (size - stop, size), 1)
            square[stop:, :] = jnp.where((lane >= start) & (lane < stop), 0.0, square[stop:, :]) - change


def solve_kernel(whole_ref, ls_ref, knobs_ref, earlier_ref, diag_ref, out_ref, res_ref,
                 table, square, kern_left, prev_left, inverse):
    step = pl.program_id(0)

    @pl.when(step == 0)
    def _():
        for piece in range(PIECES):
            row, half = (piece // 2) * PIECE_ROWS, (piece % 2) * LANES
            table[row : row + PIECE_ROWS, half : half + LANES] = whole_ref[piece]
        scaled = table[:KNOBS, :]
        earlier = table[KNOBS:, :]
        kern_left[...] = left_form(scaled.T)
        prev_left[0], prev_left[1] = split_two(earlier.T)
        eye = jnp.where(
            lax.broadcasted_iota(jnp.int32, (PIVOTS, PIVOTS), 0)
            == lax.broadcasted_iota(jnp.int32, (PIVOTS, PIVOTS), 1), 1.0, 0.0)
        square[...] = tile_of(kern_left, prev_left, scaled, earlier) + 0.5 * eye
        factor(square)
        lower = lax.broadcasted_iota(jnp.int32, (PIVOTS, PIVOTS), 0) >= lax.broadcasted_iota(
            jnp.int32, (PIVOTS, PIVOTS), 1)
        inverse[0], inverse[1] = split_two(jnp.where(lower, square[...], 0.0))

    scaled = knobs_ref[...] / column_of(ls_ref[...])
    tile = tile_of(kern_left, prev_left, scaled, earlier_ref[...])
    high, low = split_two(tile)
    inv_high = inverse[0]
    new = dot(inv_high, high) + (dot(inv_high, low) + dot(inverse[1], high))
    out_ref[...] = new
    res_ref[...] = diag_ref[...] - jnp.sum(new * new, axis=0, keepdims=True)


def collect(pivots, scale_row, knobs, earlier):
    vmem = pl.BlockSpec(memory_space=pltpu.VMEM)
    hbm = pl.BlockSpec(memory_space=pltpu.HBM)
    args = [pltpu.with_memory_space_constraint(a, pltpu.HBM) for a in (pivots, scale_row, knobs, earlier)]
    slots = lambda n: pltpu.VMEM((n, PIECE_ROWS, LANES), F32)
    dma = lambda *n: pltpu.SemaphoreType.DMA(n)
    others, chain = len(AROUND), len(ALONG)
    return pl.pallas_call(
        collect_kernel,
        out_shape=jax.ShapeDtypeStruct((PIECES, PIECE_ROWS, LANES), F32),
        in_specs=[hbm] * 4,
        out_specs=vmem,
        scratch_shapes=[
            pltpu.VMEM(pivots.shape, jnp.int32), pltpu.VMEM(scale_row.shape, F32),
            pltpu.VMEM(knobs.shape, F32), pltpu.VMEM(earlier.shape, F32),
            slots(PIECES), slots(others), slots(chain), slots(2), dma(2), dma(2, PARTS),
            dma(others), dma(others), dma(chain), dma(chain), dma(others), dma(others),
        ],
        compiler_params=pltpu.CompilerParams(
            collective_id=0, has_side_effects=True, vmem_limit_bytes=24 << 20),
        name="collect_pivots",
    )(*args)


def per_device(knobs, lengthscale, earlier, diagonal, pivots):
    count = knobs.shape[1]
    steps = count // CHUNK
    scale_row = lengthscale.reshape(1, KNOBS)
    piece_shape = (PIECES, PIECE_ROWS, LANES)
    fixed = lambda *shape: pl.BlockSpec(shape, lambda i: (0,) * len(shape))
    chunk = lambda rows: pl.BlockSpec((rows, CHUNK), lambda i: (0, i))
    whole = collect(pivots, scale_row, knobs, earlier)
    new_factor, residual = pl.pallas_call(
        solve_kernel,
        out_shape=(
            jax.ShapeDtypeStruct((PIVOTS, count), F32),
            jax.ShapeDtypeStruct((1, count), F32),
        ),
        grid=(steps,),
        in_specs=[fixed(*piece_shape), fixed(1, KNOBS), chunk(KNOBS), chunk(PREV), chunk(1)],
        out_specs=(chunk(PIVOTS), chunk(1)),
        scratch_shapes=[
            pltpu.VMEM((TABLE, PIVOTS), F32),
            pltpu.VMEM((PIVOTS, PIVOTS), F32),
            pltpu.VMEM((PIVOTS, 4 * KNOBS + 16), BF16),
            pltpu.VMEM((2, PIVOTS, PREV), BF16),
            pltpu.VMEM((2, PIVOTS, PIVOTS), BF16),
        ],
        compiler_params=pltpu.CompilerParams(vmem_limit_bytes=24 << 20),
        name="solve_columns",
    )(whole, scale_row, knobs, earlier, diagonal.reshape(1, count))
    return new_factor, residual.reshape(count)


def solution(mesh):
    in_specs = (P(None, ("rows", "sub")), P(), P(None, ("rows", "sub")), P(("rows", "sub")), P())
    out_specs = (P(None, ("rows", "sub")), P(("rows", "sub")))
    return jax.shard_map(
        per_device, mesh=mesh, in_specs=in_specs, out_specs=out_specs, check_vma=False
    )
```

```python
import jax
import jax.numpy as jnp
from jax import lax
from jax.experimental import pallas as pl
from jax.experimental.pallas import tpu as pltpu
from jax.sharding import PartitionSpec as P

MESH = pl.DeviceIdType.MESH
KNOBS, PREV, PIVOTS, LANES = 48, 256, 256, 128
TABLE = KNOBS + PREV
KERN_ROWS = 4 * KNOBS + 16
PIECES = 32
PIECE_ROWS = TABLE * (PIVOTS // LANES) // PIECES
CHUNK = 512
GROUP, WIDTH, BLOCK = 8, 16, 32
F32, BF16 = jnp.float32, jnp.bfloat16


def split_two(x):
    high = x.astype(BF16)
    return high, (x - high.astype(F32)).astype(BF16)


def split_three(x):
    high = x.astype(BF16)
    rest = x - high.astype(F32)
    mid = rest.astype(BF16)
    return high, mid, (rest - mid.astype(F32)).astype(BF16)


def dot(left, right, dims=((1,), (0,))):
    return lax.dot_general(left, right, (dims, ((), ())), preferred_element_type=F32)


def column_of(row):
    count = row.shape[1]
    square = jnp.broadcast_to(row, (count, count))
    same = lax.broadcasted_iota(jnp.int32, (count, count), 0) == lax.broadcasted_iota(
        jnp.int32, (count, count), 1
    )
    return jnp.sum(jnp.where(same, square, 0.0), axis=1, keepdims=True)


def ring(step, size):
    return min(step % size, -step % size)


AROUND = sorted(
    ((y, x, c) for y in range(4) for x in range(4) for c in range(2)),
    key=lambda t: -(4 * (ring(t[0], 4) + ring(t[1], 4)) + t[2]),
)[:-1]
NEAR, FAR, OPPOSITE = (-1, 1), (-3, 3, -6, 6), 8
ALONG = NEAR + (OPPOSITE,) + FAR
PARTS = 4


def collect_kernel(ids_hbm, ls_hbm, knobs_hbm, earlier_hbm, whole_ref, kern_right, prev_right,
                   ids_ref, ls_ref, knobs, earlier, part, rows_in, z_in, z_out,
                   small_sem, load_sem, send_a, recv_a, send_z, recv_z, send_d, recv_d):
    row, z = lax.axis_index("rows"), lax.axis_index("sub")
    subs = lax.axis_size("sub")
    core, x0, y0 = lax.rem(row, 2), lax.rem(lax.div(row, 2), 4), lax.div(row, 8)
    count = knobs_hbm.shape[1]
    width = count // PARTS

    def load(i):
        columns = pl.ds(i * width, width)
        return [
            pltpu.make_async_copy(hbm.at[:, columns], vmem.at[:, columns], load_sem.at[j, i])
            for j, (hbm, vmem) in enumerate(((knobs_hbm, knobs), (earlier_hbm, earlier)))
        ]

    def around(t, sign=1):
        dy, dx, dc = t
        y, x = lax.rem(y0 + (dy * sign) % 4, 4), lax.rem(x0 + (dx * sign) % 4, 4)
        return (y * 4 + x) * 2 + (core + dc - 2 * core * dc)

    def along(d):
        return lax.rem(z + d % subs, subs)

    small = [
        pltpu.make_async_copy(hbm, vmem, small_sem.at[j])
        for j, (hbm, vmem) in enumerate(((ids_hbm, ids_ref), (ls_hbm, ls_ref)))
    ]
    for copy in small:
        copy.start()
    for i in range(PARTS):
        for copy in load(i):
            copy.start()
    barrier = pltpu.get_barrier_semaphore()
    for t in AROUND:
        pl.semaphore_signal(barrier, inc=1, device_id=(around(t), z), device_id_type=MESH)
    for d in ALONG:
        pl.semaphore_signal(barrier, inc=1, device_id=(row, along(d)), device_id_type=MESH)

    for copy in small:
        copy.wait()
    device = row * subs + z
    ids = jnp.concatenate([ids_ref[0:1, :], ids_ref[1:2, :]], axis=1) - device * count
    scale = column_of(ls_ref[...])
    table = None
    for i in range(PARTS):
        for copy in load(i):
            copy.wait()
        columns = pl.ds(i * width, width)
        hot = lax.broadcasted_iota(jnp.int32, (width, PIVOTS), 0) == ids - i * width
        hot = jnp.where(hot, 1.0, 0.0).astype(BF16)
        scaled = knobs[:, columns] / scale
        knobs[:, columns] = scaled
        high, low = split_two(scaled)
        prev_high, prev_low = split_two(earlier[:, columns])
        prev_right[0, :, columns], prev_right[1, :, columns] = prev_high, prev_low
        high, low = jnp.concatenate([high, prev_high], axis=0), jnp.concatenate([low, prev_low], axis=0)
        found = dot(high, hot) + dot(low, hot)
        table = found if table is None else table + found
    for piece in range(PIECES):
        top, half = (piece // 2) * PIECE_ROWS, (piece % 2) * LANES
        part[piece] = table[top : top + PIECE_ROWS, half : half + LANES]
    pl.semaphore_wait(barrier, len(AROUND) + len(ALONG))

    def scatter(i):
        target = around(AROUND[i])
        return pltpu.make_async_remote_copy(
            src_ref=part.at[target], dst_ref=rows_in.at[i], send_sem=send_a.at[i], recv_sem=recv_a.at[i],
            device_id=(target, z), device_id_type=MESH)

    def pass_on(i, source):
        return pltpu.make_async_remote_copy(
            src_ref=z_out.at[source], dst_ref=z_in.at[i], send_sem=send_z.at[i], recv_sem=recv_z.at[i],
            device_id=(row, along(ALONG[i])), device_id_type=MESH)

    def spread(i, source):
        return pltpu.make_async_remote_copy(
            src_ref=whole_ref.at[source], dst_ref=whole_ref.at[source], send_sem=send_d.at[i],
            recv_sem=recv_d.at[i], device_id=(around(AROUND[i]), z), device_id_type=MESH)

    others = range(len(AROUND))
    first, second = range(len(NEAR) + 1), range(len(NEAR) + 1, len(ALONG))
    for i in others:
        scatter(i).start()
    for i in range(PARTS):
        columns = pl.ds(i * width, width)
        kern_right[:, columns] = right_form(knobs[:, columns])
    total = part[row]
    for i in reversed(others):
        scatter(i).wait_recv()
        total = total + rows_in[i]
    z_out[0] = total
    for i in first:
        pass_on(i, 0).start()
    for i in range(len(NEAR)):
        pass_on(i, 0).wait_recv()
        total = total + z_in[i]
    z_out[1] = total
    for i in second:
        pass_on(i, 1).start()
    for i in others:
        scatter(i).wait_send()
    for i in second:
        pass_on(i, 1).wait_recv()
        total = total + z_in[i]
    pass_on(len(NEAR), 0).wait_recv()
    whole_ref[row] = total + z_in[len(NEAR)]
    for i in others:
        spread(i, row).start()
    for i in first:
        pass_on(i, 0).wait_send()
    for i in second:
        pass_on(i, 1).wait_send()
    for i in reversed(others):
        spread(i, around(AROUND[i], -1)).wait_recv()
    for i in others:
        spread(i, row).wait_send()


def extended(scaled, axis):
    square = -0.5 * jnp.sum(scaled * scaled, axis=axis, keepdims=True)
    pieces = [p.astype(F32) for p in split_three(square)]
    shape = tuple(16 if d == axis else s for d, s in enumerate(scaled.shape))
    place = lax.broadcasted_iota(jnp.int32, shape, axis)

    def rows(values):
        out = jnp.zeros(shape, F32)
        for i, value in enumerate(values):
            out = jnp.where(place == i, value, out)
        return out.astype(BF16)

    high, low = split_two(scaled)
    return high, low, rows, pieces


def left_form(scaled):
    high, low, rows, pieces = extended(scaled, 1)
    return jnp.concatenate([high, high, low, low, rows(pieces + [1.0, 1.0, 1.0])], axis=1)


def right_form(scaled):
    high, low, rows, pieces = extended(scaled, 0)
    return jnp.concatenate([high, low, high, low, rows([1.0, 1.0, 1.0] + pieces)], axis=0)


def tile_of(kern_left, prev_left, kern_right, prev_high, prev_low):
    tile = jnp.exp(dot(kern_left[...], kern_right))
    left_high = prev_left[0]
    return tile - (dot(left_high, prev_high) + (dot(left_high, prev_low) + dot(prev_left[1], prev_high)))


def factor(square, between):
    size = PIVOTS
    sub = lax.broadcasted_iota(jnp.int32, (GROUP, LANES), 0)
    sub_wide = lax.broadcasted_iota(jnp.int32, (GROUP, size), 0)
    lane_wide = lax.broadcasted_iota(jnp.int32, (GROUP, size), 1)
    full = lambda v: jnp.broadcast_to(v, (GROUP, LANES))
    wide = lambda v: jnp.concatenate([v] * (size // LANES), axis=1)
    groups = BLOCK // GROUP
    for start in range(0, size, BLOCK):
        stop = start + BLOCK
        lines = [square[start + GROUP * q : start + GROUP * q + GROUP, :] for q in range(groups)]
        for left in range(0, BLOCK, WIDTH):
            first = start + left
            cols = [
                {q: full(lines[q][:, first + k : first + k + 1]) for q in range((left + k) // GROUP, groups)}
                for k in range(WIDTH)
            ]
            here = (lane_wide >= first) & (lane_wide < first + WIDTH)
            for q in range(groups):
                inside = left <= GROUP * q < left + WIDTH
                fresh = jnp.where(lane_wide - start - GROUP * q == sub_wide, 1.0, 0.0) if inside else 0.0
                lines[q] = jnp.where(here, fresh, lines[q])
            for j in range(WIDTH):
                g, at = (left + j) // GROUP, j % GROUP
                scale = lax.rsqrt(full(cols[j][g][at : at + 1, :]))
                factors = {q: cols[j][q] * scale for q in range(g, groups)}
                factors[g] = jnp.where(sub > at, factors[g], 0.0)
                for k in range(j + 1, WIDTH):
                    own = (left + k) // GROUP
                    entry = full(factors[own][k % GROUP : k % GROUP + 1, :])
                    for q in range(own, groups):
                        cols[k][q] = cols[k][q] - factors[q] * entry
                line = jnp.broadcast_to(lines[g][at : at + 1, :], (GROUP, size)) * wide(scale)
                lines[g] = jnp.where(sub_wide == at, line, lines[g] - wide(factors[g]) * line)
                for q in range(g + 1, groups):
                    lines[q] = lines[q] - wide(factors[q]) * line
        block = jnp.concatenate(lines, axis=0)
        square[start:stop, :] = block
        if stop < size:
            high, low = split_two(block)
            left = jnp.concatenate([high, high, low, low], axis=0)[:, stop:]
            right = jnp.concatenate([high, low, high, low], axis=0)
            change = dot(left, right, ((0,), (0,)))
            lane = lax.broadcasted_iota(jnp.int32, (size - stop, size), 1)
            square[stop:, :] = jnp.where((lane >= start) & (lane < stop), 0.0, square[stop:, :]) - change
        between(start // BLOCK)


def solve_kernel(whole_ref, kern_right, prev_right, diag_ref, out_hbm, res_ref,
                 table, square, kern_left, prev_left, tile, out_vmem, out_sem):
    for piece in range(PIECES):
        row, half = (piece // 2) * PIECE_ROWS, (piece % 2) * LANES
        table[row : row + PIECE_ROWS, half : half + LANES] = whole_ref[piece]
    scaled = table[:KNOBS, :]
    high, low = split_two(table[KNOBS:, :])
    kern_left[...] = left_form(scaled.T)
    prev_left[0], prev_left[1] = split_two(table[KNOBS:, :].T)
    rows = lax.broadcasted_iota(jnp.int32, (PIVOTS, PIVOTS), 0)
    columns = lax.broadcasted_iota(jnp.int32, (PIVOTS, PIVOTS), 1)
    at_pivots = tile_of(kern_left, prev_left, right_form(scaled), high, low)
    square[...] = at_pivots + jnp.where(rows == columns, 0.5, 0.0)

    count = out_hbm.shape[1]
    width = count // (PIVOTS // BLOCK)

    def between(b):
        part = pl.ds(b * width, width)
        tile[0, :, part], tile[1, :, part] = split_two(
            tile_of(kern_left, prev_left, kern_right[:, part], prev_right[0, :, part], prev_right[1, :, part]))

    factor(square, between)
    inv_high, inv_low = split_two(jnp.where(rows >= columns, square[...], 0.0))
    copies = []
    for i in range(count // CHUNK):
        part = pl.ds(i * CHUNK, CHUNK)
        new = dot(inv_high, tile[0, :, part]) + (dot(inv_high, tile[1, :, part]) + dot(inv_low, tile[0, :, part]))
        out_vmem[:, part] = new
        copies.append(pltpu.make_async_copy(out_vmem.at[:, part], out_hbm.at[:, part], out_sem.at[i]))
        copies[-1].start()
        res_ref[:, part] = diag_ref[:, part] - jnp.sum(new * new, axis=0, keepdims=True)
    for copy in copies:
        copy.wait()


def collect(pivots, scale_row, knobs, earlier):
    vmem = pl.BlockSpec(memory_space=pltpu.VMEM)
    hbm = pl.BlockSpec(memory_space=pltpu.HBM)
    args = [pltpu.with_memory_space_constraint(a, pltpu.HBM) for a in (pivots, scale_row, knobs, earlier)]
    slots = lambda n: pltpu.VMEM((n, PIECE_ROWS, LANES), F32)
    dma = lambda *n: pltpu.SemaphoreType.DMA(n)
    others, chain = len(AROUND), len(ALONG)
    return pl.pallas_call(
        collect_kernel,
        out_shape=(
            jax.ShapeDtypeStruct((PIECES, PIECE_ROWS, LANES), F32),
            jax.ShapeDtypeStruct((KERN_ROWS, knobs.shape[1]), BF16),
            jax.ShapeDtypeStruct((2,) + earlier.shape, BF16),
        ),
        in_specs=[hbm] * 4,
        out_specs=(vmem,) * 3,
        scratch_shapes=[
            pltpu.VMEM(pivots.shape, jnp.int32), pltpu.VMEM(scale_row.shape, F32),
            pltpu.VMEM(knobs.shape, F32), pltpu.VMEM(earlier.shape, F32),
            slots(PIECES), slots(others), slots(chain), slots(2), dma(2), dma(2, PARTS),
            dma(others), dma(others), dma(chain), dma(chain), dma(others), dma(others),
        ],
        compiler_params=pltpu.CompilerParams(
            collective_id=0, has_side_effects=True, vmem_limit_bytes=24 << 20),
        name="collect_pivots",
    )(*args)


def per_device(knobs, lengthscale, earlier, diagonal, pivots):
    count = knobs.shape[1]
    whole, kern_right, prev_right = collect(pivots, lengthscale.reshape(1, KNOBS), knobs, earlier)
    vmem = pl.BlockSpec(memory_space=pltpu.VMEM)
    new_factor, residual = pl.pallas_call(
        solve_kernel,
        out_shape=(
            jax.ShapeDtypeStruct((PIVOTS, count), F32),
            jax.ShapeDtypeStruct((1, count), F32),
        ),
        in_specs=[vmem] * 4,
        out_specs=(pl.BlockSpec(memory_space=pltpu.HBM), vmem),
        scratch_shapes=[
            pltpu.VMEM((TABLE, PIVOTS), F32),
            pltpu.VMEM((PIVOTS, PIVOTS), F32),
            pltpu.VMEM((PIVOTS, KERN_ROWS), BF16),
            pltpu.VMEM((2, PIVOTS, PREV), BF16),
            pltpu.VMEM((2, PIVOTS, count), BF16),
            pltpu.VMEM((PIVOTS, count), F32),
            pltpu.SemaphoreType.DMA((count // CHUNK,)),
        ],
        compiler_params=pltpu.CompilerParams(vmem_limit_bytes=24 << 20),
        name="solve_columns",
    )(whole, kern_right, prev_right, diagonal.reshape(1, count))
    return new_factor, residual.reshape(count)


def solution(mesh):
    in_specs = (P(None, ("rows", "sub")), P(), P(None, ("rows", "sub")), P(("rows", "sub")), P())
    out_specs = (P(None, ("rows", "sub")), P(("rows", "sub")))
    return jax.shard_map(
        per_device, mesh=mesh, in_specs=in_specs, out_specs=out_specs, check_vma=False
    )
```

```python
import jax
import jax.numpy as jnp
from jax import lax
from jax.experimental import pallas as pl
from jax.experimental.pallas import tpu as pltpu
from jax.sharding import PartitionSpec as P

MESH = pl.DeviceIdType.MESH
KNOBS, PREV, PIVOTS, LANES = 48, 256, 256, 128
TABLE = KNOBS + PREV
KERN_ROWS = 4 * KNOBS + 16
PIECES = 32
PIECE_ROWS = TABLE * (PIVOTS // LANES) // PIECES
CHUNK = 512
GROUP, WIDTH, BLOCK = 8, 16, 32
F32, BF16 = jnp.float32, jnp.bfloat16


def split_two(x):
    high = x.astype(BF16)
    return high, (x - high.astype(F32)).astype(BF16)


def split_three(x):
    high = x.astype(BF16)
    rest = x - high.astype(F32)
    mid = rest.astype(BF16)
    return high, mid, (rest - mid.astype(F32)).astype(BF16)


def dot(left, right, dims=((1,), (0,))):
    return lax.dot_general(left, right, (dims, ((), ())), preferred_element_type=F32)


def column_of(row):
    count = row.shape[1]
    square = jnp.broadcast_to(row, (count, count))
    same = lax.broadcasted_iota(jnp.int32, (count, count), 0) == lax.broadcasted_iota(
        jnp.int32, (count, count), 1
    )
    return jnp.sum(jnp.where(same, square, 0.0), axis=1, keepdims=True)


def ring(step, size):
    return min(step % size, -step % size)


AROUND = sorted(
    ((y, x, c) for y in range(4) for x in range(4) for c in range(2)),
    key=lambda t: -(4 * (ring(t[0], 4) + ring(t[1], 4)) + t[2]),
)[:-1]
NEAR, FAR, OPPOSITE = (-1, 1), (-3, 3, -6, 6), 8
ALONG = NEAR + (OPPOSITE,) + FAR
PARTS = 1
EARLY_ROWS = ((0, 128, 4), (128, 192, 6))


def collect_kernel(ids_hbm, ls_hbm, knobs_hbm, earlier_hbm, whole_ref, kern_right, prev_right,
                   ids_ref, ls_ref, knobs, earlier, part, rows_in, z_in, z_out,
                   small_sem, load_sem, send_a, recv_a, send_z, recv_z, send_d, recv_d):
    row, z = lax.axis_index("rows"), lax.axis_index("sub")
    subs = lax.axis_size("sub")
    core, x0, y0 = lax.rem(row, 2), lax.rem(lax.div(row, 2), 4), lax.div(row, 8)
    count = knobs_hbm.shape[1]
    width = count // PARTS

    def load(i):
        columns = pl.ds(i * width, width)
        return [
            pltpu.make_async_copy(hbm.at[:, columns], vmem.at[:, columns], load_sem.at[j, i])
            for j, (hbm, vmem) in enumerate(((knobs_hbm, knobs), (earlier_hbm, earlier)))
        ]

    def around(t, sign=1):
        dy, dx, dc = t
        y, x = lax.rem(y0 + (dy * sign) % 4, 4), lax.rem(x0 + (dx * sign) % 4, 4)
        return (y * 4 + x) * 2 + (core + dc - 2 * core * dc)

    def along(d):
        return lax.rem(z + d % subs, subs)

    small = [
        pltpu.make_async_copy(hbm, vmem, small_sem.at[j])
        for j, (hbm, vmem) in enumerate(((ids_hbm, ids_ref), (ls_hbm, ls_ref)))
    ]
    for copy in small:
        copy.start()
    for i in range(PARTS):
        for copy in load(i):
            copy.start()
    barrier = pltpu.get_barrier_semaphore()
    for t in AROUND:
        pl.semaphore_signal(barrier, inc=1, device_id=(around(t), z), device_id_type=MESH)
    for d in ALONG:
        pl.semaphore_signal(barrier, inc=1, device_id=(row, along(d)), device_id_type=MESH)

    for copy in small:
        copy.wait()
    device = row * subs + z
    ids = jnp.concatenate([ids_ref[0:1, :], ids_ref[1:2, :]], axis=1) - device * count
    scale = column_of(ls_ref[...])
    table = None
    for i in range(PARTS):
        for copy in load(i):
            copy.wait()
        columns = pl.ds(i * width, width)
        hot = lax.broadcasted_iota(jnp.int32, (width, PIVOTS), 0) == ids - i * width
        hot = jnp.where(hot, 1.0, 0.0).astype(BF16)
        scaled = knobs[:, columns] / scale
        knobs[:, columns] = scaled
        high, low = split_two(scaled)
        prev_high, prev_low = split_two(earlier[:, columns])
        prev_right[0, :, columns], prev_right[1, :, columns] = prev_high, prev_low
        high, low = jnp.concatenate([high, prev_high], axis=0), jnp.concatenate([low, prev_low], axis=0)
        found = dot(high, hot) + dot(low, hot)
        table = found if table is None else table + found
    for piece in range(PIECES):
        top, half = (piece // 2) * PIECE_ROWS, (piece % 2) * LANES
        part[piece] = table[top : top + PIECE_ROWS, half : half + LANES]
    pl.semaphore_wait(barrier, len(AROUND) + len(ALONG))

    def scatter(i):
        target = around(AROUND[i])
        return pltpu.make_async_remote_copy(
            src_ref=part.at[target], dst_ref=rows_in.at[i], send_sem=send_a.at[i], recv_sem=recv_a.at[i],
            device_id=(target, z), device_id_type=MESH)

    def pass_on(i, source):
        return pltpu.make_async_remote_copy(
            src_ref=z_out.at[source], dst_ref=z_in.at[i], send_sem=send_z.at[i], recv_sem=recv_z.at[i],
            device_id=(row, along(ALONG[i])), device_id_type=MESH)

    def spread(i, source):
        return pltpu.make_async_remote_copy(
            src_ref=whole_ref.at[source], dst_ref=whole_ref.at[source], send_sem=send_d.at[i],
            recv_sem=recv_d.at[i], device_id=(around(AROUND[i]), z), device_id_type=MESH)

    others = range(len(AROUND))
    first, second = range(len(NEAR) + 1), range(len(NEAR) + 1, len(ALONG))
    for i in others:
        scatter(i).start()
    for i in range(count // CHUNK):
        columns = pl.ds(i * CHUNK, CHUNK)
        kern_right[:, columns] = right_form(knobs[:, columns])
    total = part[row]
    for i in reversed(others):
        scatter(i).wait_recv()
        total = total + rows_in[i]
    z_out[0] = total
    for i in first:
        pass_on(i, 0).start()
    for i in range(len(NEAR)):
        pass_on(i, 0).wait_recv()
        total = total + z_in[i]
    z_out[1] = total
    for i in second:
        pass_on(i, 1).start()
    for i in others:
        scatter(i).wait_send()
    for i in second:
        pass_on(i, 1).wait_recv()
        total = total + z_in[i]
    pass_on(len(NEAR), 0).wait_recv()
    whole_ref[row] = total + z_in[len(NEAR)]
    for i in others:
        spread(i, row).start()
    for i in first:
        pass_on(i, 0).wait_send()
    for i in second:
        pass_on(i, 1).wait_send()
    for i in reversed(others):
        spread(i, around(AROUND[i], -1)).wait_recv()
    for i in others:
        spread(i, row).wait_send()


def extended(scaled, axis):
    square = -0.5 * jnp.sum(scaled * scaled, axis=axis, keepdims=True)
    pieces = [p.astype(F32) for p in split_three(square)]
    shape = tuple(16 if d == axis else s for d, s in enumerate(scaled.shape))
    place = lax.broadcasted_iota(jnp.int32, shape, axis)

    def rows(values):
        out = jnp.zeros(shape, F32)
        for i, value in enumerate(values):
            out = jnp.where(place == i, value, out)
        return out.astype(BF16)

    high, low = split_two(scaled)
    return high, low, rows, pieces


def left_form(scaled):
    high, low, rows, pieces = extended(scaled, 1)
    return jnp.concatenate([high, high, low, low, rows(pieces + [1.0, 1.0, 1.0])], axis=1)


def right_form(scaled):
    high, low, rows, pieces = extended(scaled, 0)
    return jnp.concatenate([high, low, high, low, rows([1.0, 1.0, 1.0] + pieces)], axis=0)


def tile_of(kern_left, prev_left, kern_right, prev_high, prev_low):
    tile = jnp.exp(dot(kern_left[...], kern_right))
    left_high = prev_left[0]
    return tile - (dot(left_high, prev_high) + (dot(left_high, prev_low) + dot(prev_left[1], prev_high)))


def factor(square, between):
    size = PIVOTS
    sub = lax.broadcasted_iota(jnp.int32, (GROUP, LANES), 0)
    sub_wide = lax.broadcasted_iota(jnp.int32, (GROUP, size), 0)
    lane_wide = lax.broadcasted_iota(jnp.int32, (GROUP, size), 1)
    full = lambda v: jnp.broadcast_to(v, (GROUP, LANES))
    wide = lambda v: jnp.concatenate([v] * (size // LANES), axis=1)
    entry = lambda column, row: full(column[row : row + 1, :])
    groups = BLOCK // GROUP
    for start in range(0, size, BLOCK):
        stop = start + BLOCK
        lines = [square[start + GROUP * q : start + GROUP * q + GROUP, :] for q in range(groups)]
        for left in range(0, BLOCK, WIDTH):
            first = start + left
            cols = [
                {q: full(lines[q][:, first + k : first + k + 1]) for q in range((left + k) // GROUP, groups)}
                for k in range(WIDTH)
            ]
            here = (lane_wide >= first) & (lane_wide < first + WIDTH)
            for q in range(groups):
                inside = left <= GROUP * q < left + WIDTH
                fresh = jnp.where(lane_wide - start - GROUP * q == sub_wide, 1.0, 0.0) if inside else 0.0
                lines[q] = jnp.where(here, fresh, lines[q])
            for j in range(0, WIDTH, 2):
                g, at = (left + j) // GROUP, j % GROUP
                one, two = cols[j], cols[j + 1]
                corner, side, last = entry(one[g], at), entry(one[g], at + 1), entry(two[g], at + 1)
                scale_one = lax.rsqrt(corner)
                both = scale_one * lax.rsqrt(corner * last - side * side)
                scale_two = corner * both
                one = {q: one[q] * scale_one for q in range(g, groups)}
                two = {q: (two[q] * corner - cols[j][q] * side) * both for q in range(g, groups)}
                one[g] = jnp.where(sub > at, one[g], 0.0)
                two[g] = jnp.where(sub > at + 1, two[g], 0.0)
                for k in range(j + 2, WIDTH):
                    own = (left + k) // GROUP
                    from_one, from_two = entry(one[own], k % GROUP), entry(two[own], k % GROUP)
                    for q in range(own, groups):
                        cols[k][q] = cols[k][q] - (one[q] * from_one + two[q] * from_two)
                for row, scale, factors in ((at, scale_one, one), (at + 1, scale_two, two)):
                    line = jnp.broadcast_to(lines[g][row : row + 1, :], (GROUP, size)) * wide(scale)
                    lines[g] = jnp.where(sub_wide == row, line, lines[g] - wide(factors[g]) * line)
                    for q in range(g + 1, groups):
                        lines[q] = lines[q] - wide(factors[q]) * line
        block = jnp.concatenate(lines, axis=0)
        square[start:stop, :] = block
        if stop < size:
            high, low = split_two(block)
            left = jnp.concatenate([high, high, low, low], axis=0)[:, stop:]
            right = jnp.concatenate([high, low, high, low], axis=0)
            change = dot(left, right, ((0,), (0,)))
            lane = lax.broadcasted_iota(jnp.int32, (size - stop, size), 1)
            square[stop:, :] = jnp.where((lane >= start) & (lane < stop), 0.0, square[stop:, :]) - change
        between(start // BLOCK)


def solve_kernel(whole_ref, kern_right, prev_right, diag_ref, out_hbm, res_ref,
                 table, square, kern_left, prev_left, tile, out_vmem, out_sem):
    for piece in range(PIECES):
        row, half = (piece // 2) * PIECE_ROWS, (piece % 2) * LANES
        table[row : row + PIECE_ROWS, half : half + LANES] = whole_ref[piece]
    scaled = table[:KNOBS, :]
    high, low = split_two(table[KNOBS:, :])
    kern_left[...] = left_form(scaled.T)
    prev_left[0], prev_left[1] = split_two(table[KNOBS:, :].T)
    rows = lax.broadcasted_iota(jnp.int32, (PIVOTS, PIVOTS), 0)
    columns = lax.broadcasted_iota(jnp.int32, (PIVOTS, PIVOTS), 1)
    at_pivots = tile_of(kern_left, prev_left, right_form(scaled), high, low)
    square[...] = at_pivots + jnp.where(rows == columns, 0.5, 0.0)

    count = out_hbm.shape[1]
    copies = []

    def tile_part(part):
        tile[0, :, part], tile[1, :, part] = split_two(
            tile_of(kern_left, prev_left, kern_right[:, part], prev_right[0, :, part], prev_right[1, :, part]))

    def new_rows(top, stop, parts):
        lower = rows[top:stop, :stop] >= columns[top:stop, :stop]
        inv_high, inv_low = split_two(jnp.where(lower, square[top:stop, :stop], 0.0))
        inv_both = jnp.concatenate([inv_high, inv_low], axis=0)
        for part in parts:
            both = dot(inv_both, tile[0, :stop, part])
            new = both[: stop - top] + (dot(inv_high, tile[1, :stop, part]) + both[stop - top :])
            out_vmem[top:stop, part] = new
            copies.append(pltpu.make_async_copy(
                out_vmem.at[top:stop, part], out_hbm.at[top:stop, part], out_sem.at[len(copies)]))
            copies[-1].start()
            rest = diag_ref[:, part] if top == 0 else res_ref[:, part]
            res_ref[:, part] = rest - jnp.sum(new * new, axis=0, keepdims=True)

    parts = [pl.ds(i * CHUNK, CHUNK) for i in range(count // CHUNK)]

    def between(b):
        if b < len(parts):
            tile_part(parts[b])
        for top, stop, after in EARLY_ROWS:
            if b == after:
                new_rows(top, stop, parts)

    factor(square, between)
    new_rows(EARLY_ROWS[-1][1], PIVOTS, parts)
    for copy in copies:
        copy.wait()


def collect(pivots, scale_row, knobs, earlier):
    vmem = pl.BlockSpec(memory_space=pltpu.VMEM)
    hbm = pl.BlockSpec(memory_space=pltpu.HBM)
    args = [pltpu.with_memory_space_constraint(a, pltpu.HBM) for a in (pivots, scale_row, knobs, earlier)]
    slots = lambda n: pltpu.VMEM((n, PIECE_ROWS, LANES), F32)
    dma = lambda *n: pltpu.SemaphoreType.DMA(n)
    others, chain = len(AROUND), len(ALONG)
    return pl.pallas_call(
        collect_kernel,
        out_shape=(
            jax.ShapeDtypeStruct((PIECES, PIECE_ROWS, LANES), F32),
            jax.ShapeDtypeStruct((KERN_ROWS, knobs.shape[1]), BF16),
            jax.ShapeDtypeStruct((2,) + earlier.shape, BF16),
        ),
        in_specs=[hbm] * 4,
        out_specs=(vmem,) * 3,
        scratch_shapes=[
            pltpu.VMEM(pivots.shape, jnp.int32), pltpu.VMEM(scale_row.shape, F32),
            pltpu.VMEM(knobs.shape, F32), pltpu.VMEM(earlier.shape, F32),
            slots(PIECES), slots(others), slots(chain), slots(2), dma(2), dma(2, PARTS),
            dma(others), dma(others), dma(chain), dma(chain), dma(others), dma(others),
        ],
        compiler_params=pltpu.CompilerParams(
            collective_id=0, has_side_effects=True, vmem_limit_bytes=24 << 20),
        name="collect_pivots",
    )(*args)


def per_device(knobs, lengthscale, earlier, diagonal, pivots):
    count = knobs.shape[1]
    whole, kern_right, prev_right = collect(pivots, lengthscale.reshape(1, KNOBS), knobs, earlier)
    vmem = pl.BlockSpec(memory_space=pltpu.VMEM)
    new_factor, residual = pl.pallas_call(
        solve_kernel,
        out_shape=(
            jax.ShapeDtypeStruct((PIVOTS, count), F32),
            jax.ShapeDtypeStruct((1, count), F32),
        ),
        in_specs=[vmem] * 4,
        out_specs=(pl.BlockSpec(memory_space=pltpu.HBM), vmem),
        scratch_shapes=[
            pltpu.VMEM((TABLE, PIVOTS), F32),
            pltpu.VMEM((PIVOTS, PIVOTS), F32),
            pltpu.VMEM((PIVOTS, KERN_ROWS), BF16),
            pltpu.VMEM((2, PIVOTS, PREV), BF16),
            pltpu.VMEM((2, PIVOTS, count), BF16),
            pltpu.VMEM((PIVOTS, count), F32),
            pltpu.SemaphoreType.DMA(((len(EARLY_ROWS) + 1) * (count // CHUNK),)),
        ],
        compiler_params=pltpu.CompilerParams(vmem_limit_bytes=24 << 20),
        name="solve_columns",
    )(whole, kern_right, prev_right, diagonal.reshape(1, count))
    return new_factor, residual.reshape(count)


def solution(mesh):
    in_specs = (P(None, ("rows", "sub")), P(), P(None, ("rows", "sub")), P(("rows", "sub")), P())
    out_specs = (P(None, ("rows", "sub")), P(("rows", "sub")))
    return jax.shard_map(
        per_device, mesh=mesh, in_specs=in_specs, out_specs=out_specs, check_vma=False
    )
```

```python
import jax
import jax.numpy as jnp
from jax import lax
from jax.experimental import pallas as pl
from jax.experimental.pallas import tpu as pltpu
from jax.sharding import PartitionSpec as P

MESH = pl.DeviceIdType.MESH
KNOBS, PREV, PIVOTS, LANES = 48, 256, 256, 128
TABLE = KNOBS + PREV
KERN_ROWS = 4 * KNOBS + 16
PIECES = 32
PIECE_ROWS = TABLE * (PIVOTS // LANES) // PIECES
CHUNK = 512
GROUP, WIDTH, BLOCK = 8, 16, 32
F32, BF16 = jnp.float32, jnp.bfloat16


def split_two(x):
    high = x.astype(BF16)
    return high, (x - high.astype(F32)).astype(BF16)


def split_three(x):
    high = x.astype(BF16)
    rest = x - high.astype(F32)
    mid = rest.astype(BF16)
    return high, mid, (rest - mid.astype(F32)).astype(BF16)


def dot(left, right, dims=((1,), (0,))):
    return lax.dot_general(left, right, (dims, ((), ())), preferred_element_type=F32)


def column_of(row):
    count = row.shape[1]
    square = jnp.broadcast_to(row, (count, count))
    same = lax.broadcasted_iota(jnp.int32, (count, count), 0) == lax.broadcasted_iota(
        jnp.int32, (count, count), 1
    )
    return jnp.sum(jnp.where(same, square, 0.0), axis=1, keepdims=True)


def ring(step, size):
    return min(step % size, -step % size)


AROUND = sorted(
    ((y, x, c) for y in range(4) for x in range(4) for c in range(2)),
    key=lambda t: -(4 * (ring(t[0], 4) + ring(t[1], 4)) + t[2]),
)[:-1]
NEAR, FAR, OPPOSITE = (-1, 1), (-3, 3, -6, 6), 8
ALONG = NEAR + (OPPOSITE,) + FAR
PARTS = 1
EARLY_ROWS = ((0, 128, 4), (128, 192, 6))


def collect_kernel(ids_hbm, ls_hbm, knobs_hbm, earlier_hbm, whole_ref, kern_right, prev_right,
                   ids_ref, ls_ref, knobs, earlier, part, rows_in, z_in, z_out,
                   small_sem, load_sem, send_a, recv_a, send_z, recv_z, send_d, recv_d):
    row, z = lax.axis_index("rows"), lax.axis_index("sub")
    subs = lax.axis_size("sub")
    core, x0, y0 = lax.rem(row, 2), lax.rem(lax.div(row, 2), 4), lax.div(row, 8)
    count = knobs_hbm.shape[1]
    width = count // PARTS

    def load(i):
        columns = pl.ds(i * width, width)
        return [
            pltpu.make_async_copy(hbm.at[:, columns], vmem.at[:, columns], load_sem.at[j, i])
            for j, (hbm, vmem) in enumerate(((knobs_hbm, knobs), (earlier_hbm, earlier)))
        ]

    def around(t, sign=1):
        dy, dx, dc = t
        y, x = lax.rem(y0 + (dy * sign) % 4, 4), lax.rem(x0 + (dx * sign) % 4, 4)
        return (y * 4 + x) * 2 + (core + dc - 2 * core * dc)

    def along(d):
        return lax.rem(z + d % subs, subs)

    small = [
        pltpu.make_async_copy(hbm, vmem, small_sem.at[j])
        for j, (hbm, vmem) in enumerate(((ids_hbm, ids_ref), (ls_hbm, ls_ref)))
    ]
    for copy in small:
        copy.start()
    for i in range(PARTS):
        for copy in load(i):
            copy.start()
    barrier = pltpu.get_barrier_semaphore()
    for t in AROUND:
        pl.semaphore_signal(barrier, inc=1, device_id=(around(t), z), device_id_type=MESH)
    for d in ALONG:
        pl.semaphore_signal(barrier, inc=1, device_id=(row, along(d)), device_id_type=MESH)

    for copy in small:
        copy.wait()
    device = row * subs + z
    ids = jnp.concatenate([ids_ref[0:1, :], ids_ref[1:2, :]], axis=1) - device * count
    scale = column_of(ls_ref[...])
    table = None
    for i in range(PARTS):
        for copy in load(i):
            copy.wait()
        columns = pl.ds(i * width, width)
        hot = lax.broadcasted_iota(jnp.int32, (width, PIVOTS), 0) == ids - i * width
        hot = jnp.where(hot, 1.0, 0.0).astype(BF16)
        scaled = knobs[:, columns] / scale
        knobs[:, columns] = scaled
        high, low = split_two(scaled)
        prev_high, prev_low = split_two(earlier[:, columns])
        prev_right[0, :, columns], prev_right[1, :, columns] = prev_high, prev_low
        high, low = jnp.concatenate([high, prev_high], axis=0), jnp.concatenate([low, prev_low], axis=0)
        found = dot(high, hot) + dot(low, hot)
        table = found if table is None else table + found
    for piece in range(PIECES):
        top, half = (piece // 2) * PIECE_ROWS, (piece % 2) * LANES
        part[piece] = table[top : top + PIECE_ROWS, half : half + LANES]
    pl.semaphore_wait(barrier, len(AROUND) + len(ALONG))

    def scatter(i):
        target = around(AROUND[i])
        return pltpu.make_async_remote_copy(
            src_ref=part.at[target], dst_ref=rows_in.at[i], send_sem=send_a.at[i], recv_sem=recv_a.at[i],
            device_id=(target, z), device_id_type=MESH)

    def pass_on(i, source):
        return pltpu.make_async_remote_copy(
            src_ref=z_out.at[source], dst_ref=z_in.at[i], send_sem=send_z.at[i], recv_sem=recv_z.at[i],
            device_id=(row, along(ALONG[i])), device_id_type=MESH)

    def spread(i, source):
        return pltpu.make_async_remote_copy(
            src_ref=whole_ref.at[source], dst_ref=whole_ref.at[source], send_sem=send_d.at[i],
            recv_sem=recv_d.at[i], device_id=(around(AROUND[i]), z), device_id_type=MESH)

    others = range(len(AROUND))
    first, second = range(len(NEAR) + 1), range(len(NEAR) + 1, len(ALONG))
    for i in others:
        scatter(i).start()
    for i in range(count // CHUNK):
        columns = pl.ds(i * CHUNK, CHUNK)
        kern_right[:, columns] = right_form(knobs[:, columns])
    total = part[row]
    for i in reversed(others):
        scatter(i).wait_recv()
        total = total + rows_in[i]
    z_out[0] = total
    for i in first:
        pass_on(i, 0).start()
    for i in range(len(NEAR)):
        pass_on(i, 0).wait_recv()
        total = total + z_in[i]
    z_out[1] = total
    for i in second:
        pass_on(i, 1).start()
    for i in others:
        scatter(i).wait_send()
    for i in second:
        pass_on(i, 1).wait_recv()
        total = total + z_in[i]
    pass_on(len(NEAR), 0).wait_recv()
    whole_ref[row] = total + z_in[len(NEAR)]
    for i in others:
        spread(i, row).start()
    for i in first:
        pass_on(i, 0).wait_send()
    for i in second:
        pass_on(i, 1).wait_send()
    for i in reversed(others):
        spread(i, around(AROUND[i], -1)).wait_recv()
    for i in others:
        spread(i, row).wait_send()


def extended(scaled, axis):
    high, low = split_two(scaled)
    held = high.astype(F32) + low.astype(F32)
    square = -0.5 * jnp.sum(held * held, axis=axis, keepdims=True)
    pieces = [p.astype(F32) for p in split_three(square)]
    shape = tuple(16 if d == axis else s for d, s in enumerate(scaled.shape))
    place = lax.broadcasted_iota(jnp.int32, shape, axis)

    def rows(values):
        out = jnp.zeros(shape, F32)
        for i, value in enumerate(values):
            out = jnp.where(place == i, value, out)
        return out.astype(BF16)

    return high, low, rows, pieces


def left_form(scaled):
    high, low, rows, pieces = extended(scaled, 1)
    return jnp.concatenate([high, high, low, low, rows(pieces + [1.0, 1.0, 1.0])], axis=1)


def right_form(scaled):
    high, low, rows, pieces = extended(scaled, 0)
    return jnp.concatenate([high, low, high, low, rows([1.0, 1.0, 1.0] + pieces)], axis=0)


def tile_of(kern_left, prev_left, kern_right, prev_high, prev_low):
    tile = jnp.exp(dot(kern_left[...], kern_right))
    left_high = prev_left[0]
    return tile - (dot(left_high, prev_high) + (dot(left_high, prev_low) + dot(prev_left[1], prev_high)))


def factor(square, between):
    size = PIVOTS
    sub = lax.broadcasted_iota(jnp.int32, (GROUP, LANES), 0)
    sub_wide = lax.broadcasted_iota(jnp.int32, (GROUP, size), 0)
    lane_wide = lax.broadcasted_iota(jnp.int32, (GROUP, size), 1)
    full = lambda v: jnp.broadcast_to(v, (GROUP, LANES))
    wide = lambda v: jnp.concatenate([v] * (size // LANES), axis=1)
    entry = lambda column, row: full(column[row : row + 1, :])
    groups = BLOCK // GROUP
    for start in range(0, size, BLOCK):
        stop = start + BLOCK
        lines = [square[start + GROUP * q : start + GROUP * q + GROUP, :] for q in range(groups)]
        for left in range(0, BLOCK, WIDTH):
            first = start + left
            cols = [
                {q: full(lines[q][:, first + k : first + k + 1]) for q in range((left + k) // GROUP, groups)}
                for k in range(WIDTH)
            ]
            here = (lane_wide >= first) & (lane_wide < first + WIDTH)
            for q in range(groups):
                inside = left <= GROUP * q < left + WIDTH
                fresh = jnp.where(lane_wide - start - GROUP * q == sub_wide, 1.0, 0.0) if inside else 0.0
                lines[q] = jnp.where(here, fresh, lines[q])
            for j in range(0, WIDTH, 2):
                g, at = (left + j) // GROUP, j % GROUP
                one, two = cols[j], cols[j + 1]
                corner, side, last = entry(one[g], at), entry(one[g], at + 1), entry(two[g], at + 1)
                scale_one = lax.rsqrt(corner)
                both = scale_one * lax.rsqrt(corner * last - side * side)
                scale_two = corner * both
                one = {q: one[q] * scale_one for q in range(g, groups)}
                two = {q: (two[q] * corner - cols[j][q] * side) * both for q in range(g, groups)}
                one[g] = jnp.where(sub > at, one[g], 0.0)
                two[g] = jnp.where(sub > at + 1, two[g], 0.0)
                for k in range(j + 2, WIDTH):
                    own = (left + k) // GROUP
                    from_one, from_two = entry(one[own], k % GROUP), entry(two[own], k % GROUP)
                    for q in range(own, groups):
                        cols[k][q] = cols[k][q] - (one[q] * from_one + two[q] * from_two)
                for row, scale, factors in ((at, scale_one, one), (at + 1, scale_two, two)):
                    line = jnp.broadcast_to(lines[g][row : row + 1, :], (GROUP, size)) * wide(scale)
                    lines[g] = jnp.where(sub_wide == row, line, lines[g] - wide(factors[g]) * line)
                    for q in range(g + 1, groups):
                        lines[q] = lines[q] - wide(factors[q]) * line
        block = jnp.concatenate(lines, axis=0)
        square[start:stop, :] = block
        if stop < size:
            high, low = split_two(block)
            left = jnp.concatenate([high, high, low, low], axis=0)[:, stop:]
            right = jnp.concatenate([high, low, high, low], axis=0)
            change = dot(left, right, ((0,), (0,)))
            lane = lax.broadcasted_iota(jnp.int32, (size - stop, size), 1)
            square[stop:, :] = jnp.where((lane >= start) & (lane < stop), 0.0, square[stop:, :]) - change
        between(start // BLOCK)


def solve_kernel(whole_ref, kern_right, prev_right, diag_ref, out_hbm, res_ref,
                 table, square, kern_left, prev_left, tile, out_vmem, out_sem):
    for piece in range(PIECES):
        row, half = (piece // 2) * PIECE_ROWS, (piece % 2) * LANES
        table[row : row + PIECE_ROWS, half : half + LANES] = whole_ref[piece]
    scaled = table[:KNOBS, :]
    high, low = split_two(table[KNOBS:, :])
    kern_left[...] = left_form(scaled.T)
    prev_left[0], prev_left[1] = split_two(table[KNOBS:, :].T)
    rows = lax.broadcasted_iota(jnp.int32, (PIVOTS, PIVOTS), 0)
    columns = lax.broadcasted_iota(jnp.int32, (PIVOTS, PIVOTS), 1)
    at_pivots = tile_of(kern_left, prev_left, right_form(scaled), high, low)
    square[...] = at_pivots + jnp.where(rows == columns, 0.5, 0.0)

    count = out_hbm.shape[1]
    copies = []

    def tile_part(part):
        tile[0, :, part], tile[1, :, part], tile[2, :, part] = split_three(
            tile_of(kern_left, prev_left, kern_right[:, part], prev_right[0, :, part], prev_right[1, :, part]))

    def new_rows(top, stop, parts):
        lower = rows[top:stop, :stop] >= columns[top:stop, :stop]
        inverse = split_three(jnp.where(lower, square[top:stop, :stop], 0.0))
        inv_high, inv_both = inverse[0], jnp.concatenate(inverse, axis=0)
        for part in parts:
            both, rest = dot(inv_both, tile[0, :stop, part]), dot(inv_both[: 2 * (stop - top)], tile[1, :stop, part])
            n = stop - top
            new = both[:n] + ((both[n : 2 * n] + rest[:n]) + (both[2 * n :] + rest[n:] + dot(inv_high, tile[2, :stop, part])))
            out_vmem[top:stop, part] = new
            copies.append(pltpu.make_async_copy(
                out_vmem.at[top:stop, part], out_hbm.at[top:stop, part], out_sem.at[len(copies)]))
            copies[-1].start()
            rest = diag_ref[:, part] if top == 0 else res_ref[:, part]
            res_ref[:, part] = rest - jnp.sum(new * new, axis=0, keepdims=True)

    parts = [pl.ds(i * CHUNK, CHUNK) for i in range(count // CHUNK)]

    def between(b):
        if b < len(parts):
            tile_part(parts[b])
        for top, stop, after in EARLY_ROWS:
            if b == after:
                new_rows(top, stop, parts)

    factor(square, between)
    new_rows(EARLY_ROWS[-1][1], PIVOTS, parts)
    for copy in copies:
        copy.wait()


def collect(pivots, scale_row, knobs, earlier):
    vmem = pl.BlockSpec(memory_space=pltpu.VMEM)
    hbm = pl.BlockSpec(memory_space=pltpu.HBM)
    args = [pltpu.with_memory_space_constraint(a, pltpu.HBM) for a in (pivots, scale_row, knobs, earlier)]
    slots = lambda n: pltpu.VMEM((n, PIECE_ROWS, LANES), F32)
    dma = lambda *n: pltpu.SemaphoreType.DMA(n)
    others, chain = len(AROUND), len(ALONG)
    return pl.pallas_call(
        collect_kernel,
        out_shape=(
            jax.ShapeDtypeStruct((PIECES, PIECE_ROWS, LANES), F32),
            jax.ShapeDtypeStruct((KERN_ROWS, knobs.shape[1]), BF16),
            jax.ShapeDtypeStruct((2,) + earlier.shape, BF16),
        ),
        in_specs=[hbm] * 4,
        out_specs=(vmem,) * 3,
        scratch_shapes=[
            pltpu.VMEM(pivots.shape, jnp.int32), pltpu.VMEM(scale_row.shape, F32),
            pltpu.VMEM(knobs.shape, F32), pltpu.VMEM(earlier.shape, F32),
            slots(PIECES), slots(others), slots(chain), slots(2), dma(2), dma(2, PARTS),
            dma(others), dma(others), dma(chain), dma(chain), dma(others), dma(others),
        ],
        compiler_params=pltpu.CompilerParams(
            collective_id=0, has_side_effects=True, vmem_limit_bytes=24 << 20),
        name="collect_pivots",
    )(*args)


def per_device(knobs, lengthscale, earlier, diagonal, pivots):
    count = knobs.shape[1]
    whole, kern_right, prev_right = collect(pivots, lengthscale.reshape(1, KNOBS), knobs, earlier)
    vmem = pl.BlockSpec(memory_space=pltpu.VMEM)
    new_factor, residual = pl.pallas_call(
        solve_kernel,
        out_shape=(
            jax.ShapeDtypeStruct((PIVOTS, count), F32),
            jax.ShapeDtypeStruct((1, count), F32),
        ),
        in_specs=[vmem] * 4,
        out_specs=(pl.BlockSpec(memory_space=pltpu.HBM), vmem),
        scratch_shapes=[
            pltpu.VMEM((TABLE, PIVOTS), F32),
            pltpu.VMEM((PIVOTS, PIVOTS), F32),
            pltpu.VMEM((PIVOTS, KERN_ROWS), BF16),
            pltpu.VMEM((2, PIVOTS, PREV), BF16),
            pltpu.VMEM((3, PIVOTS, count), BF16),
            pltpu.VMEM((PIVOTS, count), F32),
            pltpu.SemaphoreType.DMA(((len(EARLY_ROWS) + 1) * (count // CHUNK),)),
        ],
        compiler_params=pltpu.CompilerParams(vmem_limit_bytes=24 << 20),
        name="solve_columns",
    )(whole, kern_right, prev_right, diagonal.reshape(1, count))
    return new_factor, residual.reshape(count)


def solution(mesh):
    in_specs = (P(None, ("rows", "sub")), P(), P(None, ("rows", "sub")), P(("rows", "sub")), P())
    out_specs = (P(None, ("rows", "sub")), P(("rows", "sub")))
    return jax.shard_map(
        per_device, mesh=mesh, in_specs=in_specs, out_specs=out_specs, check_vma=False
    )
```

```python
import jax
import jax.numpy as jnp
from jax import lax
from jax.experimental import pallas as pl
from jax.experimental.pallas import tpu as pltpu
from jax.sharding import PartitionSpec as P

MESH = pl.DeviceIdType.MESH
KNOBS, PREV, PIVOTS, LANES = 48, 256, 256, 128
TABLE = KNOBS + PREV
KERN_ROWS = 4 * KNOBS + 16
PIECES = 32
PIECE_ROWS = TABLE * (PIVOTS // LANES) // PIECES
CHUNK = 512
GROUP, WIDTH, BLOCK = 8, 16, 32
F32, BF16 = jnp.float32, jnp.bfloat16


def split_two(x):
    high = x.astype(BF16)
    return high, (x - high.astype(F32)).astype(BF16)


def split_three(x):
    high = x.astype(BF16)
    rest = x - high.astype(F32)
    mid = rest.astype(BF16)
    return high, mid, (rest - mid.astype(F32)).astype(BF16)


def dot(left, right, dims=((1,), (0,))):
    return lax.dot_general(left, right, (dims, ((), ())), preferred_element_type=F32)


def column_of(row):
    count = row.shape[1]
    square = jnp.broadcast_to(row, (count, count))
    same = lax.broadcasted_iota(jnp.int32, (count, count), 0) == lax.broadcasted_iota(
        jnp.int32, (count, count), 1
    )
    return jnp.sum(jnp.where(same, square, 0.0), axis=1, keepdims=True)


def ring(step, size):
    return min(step % size, -step % size)


AROUND = sorted(
    ((y, x, c) for y in range(4) for x in range(4) for c in range(2)),
    key=lambda t: -(4 * (ring(t[0], 4) + ring(t[1], 4)) + t[2]),
)[:-1]
NEAR, FAR = (1, -1, -2), (6, 3, -3, -6)
ALONG = NEAR + FAR
GREET = (1, -1, 2, -2, 3, -3, 6, -6)
PARTS = 1
EARLY_ROWS = ((0, 128, 4), (128, 224, 6))


def collect_kernel(ids_hbm, ls_hbm, knobs_hbm, earlier_hbm, whole_ref, kern_right, prev_right,
                   ids_ref, ls_ref, knobs, earlier, part, rows_in, z_in, z_out,
                   small_sem, load_sem, send_a, recv_a, send_z, recv_z, send_d, recv_d):
    row, z = lax.axis_index("rows"), lax.axis_index("sub")
    subs = lax.axis_size("sub")
    core, x0, y0 = lax.rem(row, 2), lax.rem(lax.div(row, 2), 4), lax.div(row, 8)
    count = knobs_hbm.shape[1]
    width = count // PARTS

    def load(i):
        columns = pl.ds(i * width, width)
        return [
            pltpu.make_async_copy(hbm.at[:, columns], vmem.at[:, columns], load_sem.at[j, i])
            for j, (hbm, vmem) in enumerate(((knobs_hbm, knobs), (earlier_hbm, earlier)))
        ]

    def around(t, sign=1):
        dy, dx, dc = t
        y, x = lax.rem(y0 + (dy * sign) % 4, 4), lax.rem(x0 + (dx * sign) % 4, 4)
        return (y * 4 + x) * 2 + (core + dc - 2 * core * dc)

    def along(d):
        return lax.rem(z + d % subs, subs)

    small = [
        pltpu.make_async_copy(hbm, vmem, small_sem.at[j])
        for j, (hbm, vmem) in enumerate(((ids_hbm, ids_ref), (ls_hbm, ls_ref)))
    ]
    for copy in small:
        copy.start()
    for i in range(PARTS):
        for copy in load(i):
            copy.start()
    barrier = pltpu.get_barrier_semaphore()
    for t in AROUND:
        pl.semaphore_signal(barrier, inc=1, device_id=(around(t), z), device_id_type=MESH)
    for d in GREET:
        pl.semaphore_signal(barrier, inc=1, device_id=(row, along(d)), device_id_type=MESH)

    for copy in small:
        copy.wait()
    device = row * subs + z
    ids = jnp.concatenate([ids_ref[0:1, :], ids_ref[1:2, :]], axis=1) - device * count
    scale = column_of(ls_ref[...])
    table = None
    for i in range(PARTS):
        for copy in load(i):
            copy.wait()
        columns = pl.ds(i * width, width)
        hot = lax.broadcasted_iota(jnp.int32, (width, PIVOTS), 0) == ids - i * width
        hot = jnp.where(hot, 1.0, 0.0).astype(BF16)
        scaled = knobs[:, columns] / scale
        knobs[:, columns] = scaled
        high, low = split_two(scaled)
        prev_high, prev_low = split_two(earlier[:, columns])
        prev_right[0, :, columns], prev_right[1, :, columns] = prev_high, prev_low
        high, low = jnp.concatenate([high, prev_high], axis=0), jnp.concatenate([low, prev_low], axis=0)
        found = dot(high, hot) + dot(low, hot)
        table = found if table is None else table + found
    for piece in range(PIECES):
        top, half = (piece // 2) * PIECE_ROWS, (piece % 2) * LANES
        part[piece] = table[top : top + PIECE_ROWS, half : half + LANES]
    pl.semaphore_wait(barrier, len(AROUND) + len(GREET))

    def scatter(i):
        target = around(AROUND[i])
        return pltpu.make_async_remote_copy(
            src_ref=part.at[target], dst_ref=rows_in.at[i], send_sem=send_a.at[i], recv_sem=recv_a.at[i],
            device_id=(target, z), device_id_type=MESH)

    def pass_on(i, source):
        return pltpu.make_async_remote_copy(
            src_ref=z_out.at[source], dst_ref=z_in.at[i], send_sem=send_z.at[i], recv_sem=recv_z.at[i],
            device_id=(row, along(ALONG[i])), device_id_type=MESH)

    def spread(i, source):
        return pltpu.make_async_remote_copy(
            src_ref=whole_ref.at[source], dst_ref=whole_ref.at[source], send_sem=send_d.at[i],
            recv_sem=recv_d.at[i], device_id=(around(AROUND[i]), z), device_id_type=MESH)

    others = range(len(AROUND))
    first, second = range(len(NEAR)), range(len(NEAR), len(ALONG))
    for i in others:
        scatter(i).start()
    for i in range(count // CHUNK):
        columns = pl.ds(i * CHUNK, CHUNK)
        kern_right[:, columns] = right_form(knobs[:, columns])
    total = part[row]
    for i in reversed(others):
        scatter(i).wait_recv()
        total = total + rows_in[i]
    z_out[0] = total
    for i in first:
        pass_on(i, 0).start()
    for i in first[:-1]:
        pass_on(i, 0).wait_recv()
        total = total + z_in[i]
    z_out[1] = total
    for i in second[:-1]:
        pass_on(i, 1).start()
    pass_on(first[-1], 0).wait_recv()
    z_out[2] = total + z_in[first[-1]]
    pass_on(second[-1], 2).start()
    for i in others:
        scatter(i).wait_send()
    for i in second:
        pass_on(i, 1).wait_recv()
        total = total + z_in[i]
    whole_ref[row] = total
    for i in others:
        spread(i, row).start()
    for i in first:
        pass_on(i, 0).wait_send()
    for i in second:
        pass_on(i, 2 if i == second[-1] else 1).wait_send()
    for i in reversed(others):
        spread(i, around(AROUND[i], -1)).wait_recv()
    for i in others:
        spread(i, row).wait_send()


def extended(scaled, axis):
    high, low = split_two(scaled)
    held = high.astype(F32) + low.astype(F32)
    square = -0.5 * jnp.sum(held * held, axis=axis, keepdims=True)
    pieces = [p.astype(F32) for p in split_three(square)]
    shape = tuple(16 if d == axis else s for d, s in enumerate(scaled.shape))
    place = lax.broadcasted_iota(jnp.int32, shape, axis)

    def rows(values):
        out = jnp.zeros(shape, F32)
        for i, value in enumerate(values):
            out = jnp.where(place == i, value, out)
        return out.astype(BF16)

    return high, low, rows, pieces


def left_form(scaled):
    high, low, rows, pieces = extended(scaled, 1)
    return jnp.concatenate([high, high, low, low, rows(pieces + [1.0, 1.0, 1.0])], axis=1)


def right_form(scaled):
    high, low, rows, pieces = extended(scaled, 0)
    return jnp.concatenate([high, low, high, low, rows([1.0, 1.0, 1.0] + pieces)], axis=0)


def tile_of(kern_left, prev_left, kern_right, prev_high, prev_low):
    tile = jnp.exp(dot(kern_left[...], kern_right))
    left_high = prev_left[0]
    return tile - (dot(left_high, prev_high) + (dot(left_high, prev_low) + dot(prev_left[1], prev_high)))


def factor(square, between):
    size = PIVOTS
    sub = lax.broadcasted_iota(jnp.int32, (GROUP, LANES), 0)
    sub_wide = lax.broadcasted_iota(jnp.int32, (GROUP, size), 0)
    lane_wide = lax.broadcasted_iota(jnp.int32, (GROUP, size), 1)
    full = lambda v: jnp.broadcast_to(v, (GROUP, LANES))
    wide = lambda v: jnp.concatenate([v] * (size // LANES), axis=1)
    entry = lambda column, row: full(column[row : row + 1, :])
    groups = BLOCK // GROUP
    for start in range(0, size, BLOCK):
        stop = start + BLOCK
        lines = [square[start + GROUP * q : start + GROUP * q + GROUP, :] for q in range(groups)]
        for left in range(0, BLOCK, WIDTH):
            first = start + left
            cols = [
                {q: full(lines[q][:, first + k : first + k + 1]) for q in range((left + k) // GROUP, groups)}
                for k in range(WIDTH)
            ]
            here = (lane_wide >= first) & (lane_wide < first + WIDTH)
            for q in range(groups):
                inside = left <= GROUP * q < left + WIDTH
                fresh = jnp.where(lane_wide - start - GROUP * q == sub_wide, 1.0, 0.0) if inside else 0.0
                lines[q] = jnp.where(here, fresh, lines[q])
            for j in range(0, WIDTH, 2):
                g, at = (left + j) // GROUP, j % GROUP
                one, two = cols[j], cols[j + 1]
                corner, side, last = entry(one[g], at), entry(one[g], at + 1), entry(two[g], at + 1)
                scale_one = lax.rsqrt(corner)
                both = scale_one * lax.rsqrt(corner * last - side * side)
                scale_two = corner * both
                one = {q: one[q] * scale_one for q in range(g, groups)}
                two = {q: (two[q] * corner - cols[j][q] * side) * both for q in range(g, groups)}
                one[g] = jnp.where(sub > at, one[g], 0.0)
                two[g] = jnp.where(sub > at + 1, two[g], 0.0)
                for k in range(j + 2, WIDTH):
                    own = (left + k) // GROUP
                    from_one, from_two = entry(one[own], k % GROUP), entry(two[own], k % GROUP)
                    for q in range(own, groups):
                        cols[k][q] = cols[k][q] - (one[q] * from_one + two[q] * from_two)
                for row, scale, factors in ((at, scale_one, one), (at + 1, scale_two, two)):
                    line = jnp.broadcast_to(lines[g][row : row + 1, :], (GROUP, size)) * wide(scale)
                    lines[g] = jnp.where(sub_wide == row, line, lines[g] - wide(factors[g]) * line)
                    for q in range(g + 1, groups):
                        lines[q] = lines[q] - wide(factors[q]) * line
        block = jnp.concatenate(lines, axis=0)
        square[start:stop, :] = block
        if stop < size:
            high, low = split_two(block)
            left = jnp.concatenate([high, high, low, low], axis=0)[:, stop:]
            right = jnp.concatenate([high, low, high, low], axis=0)
            change = dot(left, right, ((0,), (0,)))
            lane = lax.broadcasted_iota(jnp.int32, (size - stop, size), 1)
            square[stop:, :] = jnp.where((lane >= start) & (lane < stop), 0.0, square[stop:, :]) - change
        between(start // BLOCK)


def solve_kernel(whole_ref, kern_right, prev_right, diag_ref, out_hbm, res_ref,
                 table, square, kern_left, prev_left, tile, out_vmem, out_sem):
    for piece in range(PIECES):
        row, half = (piece // 2) * PIECE_ROWS, (piece % 2) * LANES
        table[row : row + PIECE_ROWS, half : half + LANES] = whole_ref[piece]
    scaled = table[:KNOBS, :]
    high, low = split_two(table[KNOBS:, :])
    kern_left[...] = left_form(scaled.T)
    prev_left[0], prev_left[1] = split_two(table[KNOBS:, :].T)
    rows = lax.broadcasted_iota(jnp.int32, (PIVOTS, PIVOTS), 0)
    columns = lax.broadcasted_iota(jnp.int32, (PIVOTS, PIVOTS), 1)
    at_pivots = tile_of(kern_left, prev_left, right_form(scaled), high, low)
    square[...] = at_pivots + jnp.where(rows == columns, 0.5, 0.0)

    count = out_hbm.shape[1]
    copies = []

    def tile_part(part):
        tile[0, :, part], tile[1, :, part], tile[2, :, part] = split_three(
            tile_of(kern_left, prev_left, kern_right[:, part], prev_right[0, :, part], prev_right[1, :, part]))

    def new_rows(top, stop, parts):
        lower = rows[top:stop, :stop] >= columns[top:stop, :stop]
        inverse = split_three(jnp.where(lower, square[top:stop, :stop], 0.0))
        inv_high, inv_both = inverse[0], jnp.concatenate(inverse, axis=0)
        for part in parts:
            both, rest = dot(inv_both, tile[0, :stop, part]), dot(inv_both[: 2 * (stop - top)], tile[1, :stop, part])
            n = stop - top
            new = both[:n] + ((both[n : 2 * n] + rest[:n]) + (both[2 * n :] + rest[n:] + dot(inv_high, tile[2, :stop, part])))
            out_vmem[top:stop, part] = new
            copies.append(pltpu.make_async_copy(
                out_vmem.at[top:stop, part], out_hbm.at[top:stop, part], out_sem.at[len(copies)]))
            copies[-1].start()
            rest = diag_ref[:, part] if top == 0 else res_ref[:, part]
            res_ref[:, part] = rest - jnp.sum(new * new, axis=0, keepdims=True)

    parts = [pl.ds(i * CHUNK, CHUNK) for i in range(count // CHUNK)]

    def between(b):
        if b < len(parts):
            tile_part(parts[b])
        for top, stop, after in EARLY_ROWS:
            if b == after:
                new_rows(top, stop, parts)

    factor(square, between)
    new_rows(EARLY_ROWS[-1][1], PIVOTS, parts)
    for copy in copies:
        copy.wait()


def collect(pivots, scale_row, knobs, earlier):
    vmem = pl.BlockSpec(memory_space=pltpu.VMEM)
    hbm = pl.BlockSpec(memory_space=pltpu.HBM)
    args = [pltpu.with_memory_space_constraint(a, pltpu.HBM) for a in (pivots, scale_row, knobs, earlier)]
    slots = lambda n: pltpu.VMEM((n, PIECE_ROWS, LANES), F32)
    dma = lambda *n: pltpu.SemaphoreType.DMA(n)
    others, chain = len(AROUND), len(ALONG)
    return pl.pallas_call(
        collect_kernel,
        out_shape=(
            jax.ShapeDtypeStruct((PIECES, PIECE_ROWS, LANES), F32),
            jax.ShapeDtypeStruct((KERN_ROWS, knobs.shape[1]), BF16),
            jax.ShapeDtypeStruct((2,) + earlier.shape, BF16),
        ),
        in_specs=[hbm] * 4,
        out_specs=(vmem,) * 3,
        scratch_shapes=[
            pltpu.VMEM(pivots.shape, jnp.int32), pltpu.VMEM(scale_row.shape, F32),
            pltpu.VMEM(knobs.shape, F32), pltpu.VMEM(earlier.shape, F32),
            slots(PIECES), slots(others), slots(chain), slots(3), dma(2), dma(2, PARTS),
            dma(others), dma(others), dma(chain), dma(chain), dma(others), dma(others),
        ],
        compiler_params=pltpu.CompilerParams(
            collective_id=0, has_side_effects=True, vmem_limit_bytes=24 << 20),
        name="collect_pivots",
    )(*args)


def per_device(knobs, lengthscale, earlier, diagonal, pivots):
    count = knobs.shape[1]
    whole, kern_right, prev_right = collect(pivots, lengthscale.reshape(1, KNOBS), knobs, earlier)
    vmem = pl.BlockSpec(memory_space=pltpu.VMEM)
    new_factor, residual = pl.pallas_call(
        solve_kernel,
        out_shape=(
            jax.ShapeDtypeStruct((PIVOTS, count), F32),
            jax.ShapeDtypeStruct((1, count), F32),
        ),
        in_specs=[vmem] * 4,
        out_specs=(pl.BlockSpec(memory_space=pltpu.HBM), vmem),
        scratch_shapes=[
            pltpu.VMEM((TABLE, PIVOTS), F32),
            pltpu.VMEM((PIVOTS, PIVOTS), F32),
            pltpu.VMEM((PIVOTS, KERN_ROWS), BF16),
            pltpu.VMEM((2, PIVOTS, PREV), BF16),
            pltpu.VMEM((3, PIVOTS, count), BF16),
            pltpu.VMEM((PIVOTS, count), F32),
            pltpu.SemaphoreType.DMA(((len(EARLY_ROWS) + 1) * (count // CHUNK),)),
        ],
        compiler_params=pltpu.CompilerParams(vmem_limit_bytes=24 << 20),
        name="solve_columns",
    )(whole, kern_right, prev_right, diagonal.reshape(1, count))
    return new_factor, residual.reshape(count)


def solution(mesh):
    in_specs = (P(None, ("rows", "sub")), P(), P(None, ("rows", "sub")), P(("rows", "sub")), P())
    out_specs = (P(None, ("rows", "sub")), P(("rows", "sub")))
    return jax.shard_map(
        per_device, mesh=mesh, in_specs=in_specs, out_specs=out_specs, check_vma=False
    )
```
